32 devices in a mesh: dev: 4 (over z), ha: 4 (over y, x), wa: 2 (over core).
Axes of the slice: x: 2, y: 2, z: 4, core: 2. Of those that a mesh axis runs over, the one named last changes fastest.
Arguments:
- volume: float32 [16, 32, 16, 256], P('dev', 'ha', 'wa'), may hold values from -6 to 6
- kernel: float32 [256, 27, 256], replicated, may hold values from -0.078125 to 0.078125
- upstream: float32 [16, 32, 16, 256], P('dev', 'ha', 'wa'), may hold values from -6 to 6
Outputs:
- output: float32 [16, 32, 16, 256], P('dev', 'ha', 'wa')
- volume_grad: float32 [16, 32, 16, 256], P('dev', 'ha', 'wa')
- kernel_grad: float32 [256, 27, 256], P('wa')
The draws below stay inside these ranges and needn't reach their ends.
All inputs are finite; a program needn't handle non-finite values.
Results may differ from the reference program's by a relative error of at most 0.0001.
Values sent between devices are 32-bit elements; how exact they have to be, the bound alone decides.
No kernel may reach another device: no remote copies, remote signals or barrier semaphores. Data moves between devices by JAX's collectives and lax.ppermute only.
A program may use at most 128 MiB of HBM per device.

```python
import math
import jax
import jax.numpy as jnp
from jax import lax

C = 256
TAPS = 27
DEPTH = 16
HEIGHT = 32
WIDTH = 16


def shard_levels(key, shape, shards, least, largest):
    def one(position, shards_of):
        draws = jax.random.uniform(jax.random.fold_in(jax.random.fold_in(key, 6), position), (shards_of,), jnp.float32, least / len(shards), largest / len(shards))
        return jnp.repeat(jnp.exp(draws), shape[position] // shards_of).reshape((-1,) + (1,) * (len(shape) - position - 1))

    factor_of = one(*shards[0])
    for cut in shards[1:]:
        factor_of = factor_of * one(*cut)
    return factor_of


def noise(rng, extent, width, reach, split=(), dtype=jnp.bfloat16):
    gain = shard_levels(rng, extent, split, -0.22, 0.18) if split else 1.0
    drawn = jax.random.normal(rng, extent, jnp.float32) * width * gain
    return jnp.minimum(jnp.maximum(drawn, -reach), reach).astype(dtype)


def setup_inputs(seed: int = 0) -> dict:
    arg_keys = jax.random.split(jax.random.key(seed), 4)
    volume = noise(arg_keys[0], (DEPTH, HEIGHT, WIDTH, C), 1.0, 6.0, ((0, 4), (1, 4), (2, 2)), jnp.float32)
    kernel = noise(arg_keys[1], (C, TAPS, C), (C * TAPS) ** -0.5, 0.078125, (), jnp.float32)
    upstream = noise(arg_keys[2], (DEPTH, HEIGHT, WIDTH, C), 1.0, 6.0, ((0, 4), (1, 4), (2, 2)), jnp.float32)
    return dict(volume=volume, kernel=kernel, upstream=upstream)


def tap_offsets():
    return [(da, db, dc) for da in (-1, 0, 1) for db in (-1, 0, 1) for dc in (-1, 0, 1)]

def reference(volume, kernel, upstream):
    cells = DEPTH * HEIGHT * WIDTH
    flat_up = upstream.reshape(cells, C)
    output = jnp.zeros((cells, C), jnp.float32)
    volume_grad = jnp.zeros((cells, C), jnp.float32)
    grads = []
    for tap_index, (da, db, dc) in enumerate(tap_offsets()):
        shifted = jnp.roll(volume, (-da, -db, -dc), axis=(0, 1, 2)).reshape(cells, C)
        weight = kernel[:, tap_index, :]
        output = output + jnp.dot(shifted, weight, precision=lax.Precision.HIGHEST, preferred_element_type=jnp.float32)
        back = jnp.roll(upstream, (da, db, dc), axis=(0, 1, 2)).reshape(cells, C)
        volume_grad = volume_grad + jnp.dot(back, weight.T, precision=lax.Precision.HIGHEST, preferred_element_type=jnp.float32)
        grads.append(jnp.dot(shifted.T, flat_up, precision=lax.Precision.HIGHEST, preferred_element_type=jnp.float32))
    kernel_grad = jnp.stack(grads, axis=1) * (1.0 / math.sqrt(cells))
    return (output.reshape(DEPTH, HEIGHT, WIDTH, C), volume_grad.reshape(DEPTH, HEIGHT, WIDTH, C), kernel_grad)
```

```python
import functools
import math

import jax
import jax.numpy as jnp
from jax import lax
from jax.experimental import pallas as pl
from jax.experimental.pallas import tpu as pltpu
from jax.sharding import PartitionSpec as P

F32, BF16 = jnp.float32, jnp.bfloat16


def split(x):
    hi = x.astype(BF16)
    return hi, (x - hi.astype(F32)).astype(BF16)


def padded_by_halo(shard, sides):
    for axis, dim in sides:
        count, length = lax.axis_size(axis), shard.shape[dim]
        up = [(i, (i + 1) % count) for i in range(count)]
        down = [(j, i) for i, j in up]
        before = lax.ppermute(lax.slice_in_dim(shard, length - 1, length, axis=dim), axis, up)
        after = lax.ppermute(lax.slice_in_dim(shard, 0, 1, axis=dim), axis, down)
        shard = jnp.concatenate([before, shard, after], axis=dim)
    return shard


def plain(volume, kernel, upstream):
    depth, height, width, channels = volume.shape
    cells = depth * height * width
    padded = padded_by_halo(jnp.stack([volume, upstream]), (("dev", 1), ("ha", 2), ("wa", 3)))

    def windows(which, sign):
        return jnp.stack(
            [
                padded[which, 1 + sign * a :, 1 + sign * b :, 1 + sign * c :][:depth, :height, :width].reshape(cells, channels)
                for a in (-1, 0, 1) for b in (-1, 0, 1) for c in (-1, 0, 1)
            ],
            axis=1,
        )

    dot = functools.partial(jnp.einsum, precision=lax.Precision.HIGHEST, preferred_element_type=F32)
    forward, backward = windows(0, 1), windows(1, -1)
    output = dot("ntc,cto->no", forward, kernel)
    volume_grad = dot("nto,cto->nc", backward, kernel)
    total = cells * lax.axis_size("dev") * lax.axis_size("ha") * lax.axis_size("wa")
    summed = lax.psum(dot("ntc,no->cto", forward, upstream.reshape(cells, channels)) * (1.0 / math.sqrt(total)), ("dev", "ha", "wa"))
    owned = channels // lax.axis_size("wa")
    kernel_grad = lax.dynamic_slice_in_dim(summed, lax.axis_index("wa") * owned, owned, 0)
    return output.reshape(volume.shape), volume_grad.reshape(volume.shape), kernel_grad


def conv_kernel(v_ref, u_ref, k_ref, out_ref, grad_ref):
    step = pl.program_id(0)
    a, b = step // 3, step % 3

    @pl.when(step == 0)
    def _():
        out_ref[...] = jnp.zeros_like(out_ref)
        grad_ref[...] = jnp.zeros_like(grad_ref)

    cells, channels = out_ref.shape
    d, h = v_ref.shape[1] - 2, v_ref.shape[2] - 2
    out, grad = out_ref[...], grad_ref[...]
    for c in range(3):
        k_hi, k_lo = split(k_ref[c])
        v_hi, v_lo = split(v_ref[c, pl.ds(a, d), pl.ds(b, h)].reshape(cells, channels))
        u_hi, u_lo = split(u_ref[2 - c, pl.ds(2 - a, d), pl.ds(2 - b, h)].reshape(cells, channels))
        for left, right in ((v_hi, k_hi), (v_hi, k_lo), (v_lo, k_hi)):
            out += jnp.dot(left, right, preferred_element_type=F32)
        for left, right in ((u_hi, k_hi), (u_hi, k_lo), (u_lo, k_hi)):
            grad += lax.dot_general(left, right, (((1,), (1,)), ((), ())), preferred_element_type=F32)
    out_ref[...] = out
    grad_ref[...] = grad


def shifted_3(padded):
    width = padded.shape[2] - 2
    return jnp.stack([padded[:, :, c : c + width] for c in range(3)])


def conv_both(volume_padded, upstream_padded, taps):
    v, u = shifted_3(volume_padded), shifted_3(upstream_padded)
    cells = (v.shape[1] - 2) * (v.shape[2] - 2) * v.shape[3]
    channels = v.shape[4]
    whole = pl.BlockSpec(v.shape, lambda i: (0,) * 5)
    result = pl.BlockSpec((cells, channels), lambda i: (0, 0))
    shape = jax.ShapeDtypeStruct((cells, channels), F32)
    return pl.pallas_call(
        conv_kernel,
        grid=(9,),
        in_specs=[whole, whole, pl.BlockSpec((3, channels, channels), lambda i: (i, 0, 0))],
        out_specs=[result, result],
        out_shape=[shape, shape],
        compiler_params=pltpu.CompilerParams(vmem_limit_bytes=40 * 2**20),
        cost_estimate=pl.CostEstimate(flops=2 * 6 * 27 * cells * channels * channels, bytes_accessed=9 * 2**20, transcendentals=0),
        name="conv_both",
    )(v, u, taps)


def plane_grad_kernel(scale, mine_ref, sibling_ref, *refs):
    u_refs, out_ref, shifted, u_cat = refs[:8], refs[8], refs[9], refs[10]
    lane = lax.broadcasted_iota(jnp.int32, (32, 8, 128), 2)
    row = lax.broadcasted_iota(jnp.int32, (32, 8, 128), 1)
    for half in range(2):
        for z in range(3):
            mine = mine_ref[:, z].reshape(32, 8, 128)
            other = sibling_ref[:, z].reshape(32, 8, 128)
            first = pltpu.roll(mine, (128 - 32 * half) % 128, 2)
            second = pltpu.roll(other, 64 - 32 * half, 2)
            first = jnp.where(lane < 32, first, 0.0)
            second = jnp.where(lane < 32, second, 0.0)
            down_1, down_2 = pltpu.roll(first, 1, 1), pltpu.roll(second, 1, 1)
            up_1, up_2 = pltpu.roll(first, 7, 1), pltpu.roll(second, 7, 1)
            for w, (before, here, after) in enumerate(
                (
                    (jnp.where(row == 0, down_2, down_1), first, jnp.where(row == 7, up_2, up_1)),
                    (jnp.where(row == 0, down_1, down_2), second, jnp.where(row == 7, up_1, up_2)),
                )
            ):
                joined = before + pltpu.roll(here, 32, 2) + pltpu.roll(after, 64, 2)
                plane = 3 * half + z
                shifted[w, plane, pl.ds(1, 32)] = joined
                shifted[w, plane, 0] = joined[31]
                shifted[w, plane, 33] = joined[0]
    for i, u_ref in enumerate(u_refs):
        hi, lo = split(u_ref[...].T)
        u_cat[i, :, 0:256] = hi
        u_cat[i, :, 256:512] = hi
        u_cat[i, :, 512:768] = lo
    windows = [(a, b) for a in range(3) for b in range(3)]
    for first in range(0, 9, 2):
        group = windows[first : first + 2]
        total = jnp.zeros((256, 128 * len(group)), F32)
        for w in range(2):
            for k in range(4):
                cells = [shifted[w, a : a + 4, 8 * k + b : 8 * k + b + 8].reshape(256, 128) for a, b in group]
                cells = jnp.concatenate(cells, axis=1)
                hi, lo = split(cells)
                right = jnp.concatenate([hi, lo, hi], axis=0)
                total += jnp.dot(u_cat[4 * w + k], right, preferred_element_type=F32)
        turned = total.T * scale
        for i, (a, b) in enumerate(group):
            for c in range(3):
                out_ref[9 * a + 3 * b + c] = turned[128 * i + 32 * c : 128 * i + 32 * c + 32]


def plane_grad(mine, sibling, u_blocks, scale):
    return pl.pallas_call(
        functools.partial(plane_grad_kernel, scale),
        out_shape=jax.ShapeDtypeStruct((27, 32, 256), F32),
        in_specs=[pl.BlockSpec(memory_space=pltpu.VMEM)] * 10,
        out_specs=pl.BlockSpec(memory_space=pltpu.VMEM),
        scratch_shapes=[pltpu.VMEM((2, 6, 34, 8, 128), F32), pltpu.VMEM((8, 256, 768), BF16)],
        compiler_params=pltpu.CompilerParams(vmem_limit_bytes=40 * 2**20),
        cost_estimate=pl.CostEstimate(flops=2 * 3 * 27 * 32 * 2048 * 256, bytes_accessed=4 * 2**20, transcendentals=0),
        name="plane_grad",
    )(mine, sibling, *u_blocks)


SWAP = [(0, 1), (1, 0)]
UP = [(i, (i + 1) % 4) for i in range(4)]
DOWN = [((i + 1) % 4, i) for i in range(4)]


def pair(bit):
    return [(i, i ^ bit) for i in range(4)]


def sum_over_dev(x):
    return lax.psum(x, "dev")


def gather_over_ha(x, order):
    first, second = order
    got = lax.ppermute(x, "ha", pair(first))
    both = lax.ppermute(jnp.stack([x, got]), "ha", pair(second))
    return {0: x, first: got, second: both[0], first ^ second: both[1]}


def shared(volume, kernel, upstream):
    h, w = lax.axis_index("ha"), lax.axis_index("wa")
    channels = volume.shape[-1]
    taps = kernel.transpose(1, 0, 2)
    scale = 1.0 / math.sqrt(256 * 32)

    u_flat = upstream.reshape(256, channels)
    u_own = [u_flat] + [lax.ppermute(u_flat, "ha", [((i + k) % 4, i) for i in range(4)]) for k in (1, 2, 3)]
    u_other = [lax.ppermute(x, "wa", SWAP) for x in u_own]

    below = lax.ppermute(volume[3:4], "dev", UP)
    above = lax.ppermute(volume[0:1], "dev", DOWN)
    v_deep = jnp.concatenate([below, volume, above], axis=0)
    parts = v_deep.reshape(2, 192, 2, 4, 32)
    parts = jnp.where(w == 0, parts, parts[:, :, ::-1])
    parts = parts.transpose(3, 1, 2, 0, 4).reshape(4, 192, 128)

    def for_chip(k):
        return lax.dynamic_index_in_dim(parts, lax.rem(h + k, 4), 0, keepdims=False)

    v_own = [for_chip(0)] + [lax.ppermute(for_chip(4 - k), "ha", [((i + k) % 4, i) for i in range(4)]) for k in (1, 2, 3)]
    v_own = jnp.stack(v_own)
    v_other = lax.ppermute(v_own, "wa", SWAP)
    packed = (4, 3, 8, 8, 128)
    piece = plane_grad(v_own.reshape(packed), v_other.reshape(packed), u_own + u_other, scale)

    kernel_grad = jnp.zeros((27, 128, channels), F32)
    for i in range(3):
        whole = sum_over_dev(piece[9 * i : 9 * i + 9])
        for s, x in gather_over_ha(whole, (1, 2) if i % 2 == 0 else (2, 1)).items():
            kernel_grad = lax.dynamic_update_slice(kernel_grad, x, (9 * i, 32 * (h ^ s), 0))
    kernel_grad = kernel_grad.transpose(1, 0, 2)

    behind = lax.ppermute(v_deep[:, 7:8], "ha", UP)
    ahead = lax.ppermute(v_deep[:, 0:1], "ha", DOWN)
    v_rows = jnp.concatenate([behind, v_deep, ahead], axis=1)
    sides = lax.ppermute(jnp.concatenate([v_rows[:, :, 7:8], v_rows[:, :, 0:1]], axis=2), "wa", SWAP)
    v_padded = jnp.concatenate([sides[:, :, 0:1], v_rows, sides[:, :, 1:2]], axis=2)

    def rows(blocks):
        blocks = [x.reshape(4, 8, 8, channels) for x in blocks]
        return jnp.concatenate([blocks[3][:, 7:8], blocks[0], blocks[1][:, 0:1]], axis=1)

    mine, other = rows(u_own), rows(u_other)
    u_flat_padded = jnp.concatenate([other[:, :, 7:8], mine, other[:, :, 0:1]], axis=2)
    u_below = lax.ppermute(u_flat_padded[3:4], "dev", UP)
    u_above = lax.ppermute(u_flat_padded[0:1], "dev", DOWN)
    u_padded = jnp.concatenate([u_below, u_flat_padded, u_above], axis=0)
    output, volume_grad = conv_both(v_padded, u_padded, taps)
    return output.reshape(volume.shape), volume_grad.reshape(volume.shape), kernel_grad


def solution(mesh):
    sizes = tuple(mesh.shape[name] for name in ("dev", "ha", "wa"))
    placed = (P("dev", "ha", "wa", None), P(), P("dev", "ha", "wa", None))

    def per_device(volume, kernel, upstream):
        fits = sizes == (4, 4, 2) and volume.shape == (4, 8, 8, 256) and kernel.shape == (256, 27, 256)
        return (shared if fits else plain)(volume, kernel, upstream)

    return jax.shard_map(
        per_device,
        mesh=mesh,
        in_specs=placed,
        out_specs=(P("dev", "ha", "wa", None), P("dev", "ha", "wa", None), P("wa", None, None)),
        check_vma=False,
    )
```

```python
import functools
import math

import jax
import jax.numpy as jnp
from jax import lax
from jax.experimental import pallas as pl
from jax.experimental.pallas import tpu as pltpu
from jax.sharding import PartitionSpec as P

F32, BF16 = jnp.float32, jnp.bfloat16


def split(x):
    hi = x.astype(BF16)
    return hi, (x - hi.astype(F32)).astype(BF16)


def padded_by_halo(shard, sides):
    for axis, dim in sides:
        count, length = lax.axis_size(axis), shard.shape[dim]
        up = [(i, (i + 1) % count) for i in range(count)]
        down = [(j, i) for i, j in up]
        before = lax.ppermute(lax.slice_in_dim(shard, length - 1, length, axis=dim), axis, up)
        after = lax.ppermute(lax.slice_in_dim(shard, 0, 1, axis=dim), axis, down)
        shard = jnp.concatenate([before, shard, after], axis=dim)
    return shard


def plain(volume, kernel, upstream):
    depth, height, width, channels = volume.shape
    cells = depth * height * width
    padded = padded_by_halo(jnp.stack([volume, upstream]), (("dev", 1), ("ha", 2), ("wa", 3)))

    def windows(which, sign):
        return jnp.stack(
            [
                padded[which, 1 + sign * a :, 1 + sign * b :, 1 + sign * c :][:depth, :height, :width].reshape(cells, channels)
                for a in (-1, 0, 1) for b in (-1, 0, 1) for c in (-1, 0, 1)
            ],
            axis=1,
        )

    dot = functools.partial(jnp.einsum, precision=lax.Precision.HIGHEST, preferred_element_type=F32)
    forward, backward = windows(0, 1), windows(1, -1)
    output = dot("ntc,cto->no", forward, kernel)
    volume_grad = dot("nto,cto->nc", backward, kernel)
    total = cells * lax.axis_size("dev") * lax.axis_size("ha") * lax.axis_size("wa")
    summed = lax.psum(dot("ntc,no->cto", forward, upstream.reshape(cells, channels)) * (1.0 / math.sqrt(total)), ("dev", "ha", "wa"))
    owned = channels // lax.axis_size("wa")
    kernel_grad = lax.dynamic_slice_in_dim(summed, lax.axis_index("wa") * owned, owned, 0)
    return output.reshape(volume.shape), volume_grad.reshape(volume.shape), kernel_grad


def conv_kernel(a, *refs):
    v_refs, u_refs, k_ref, out_ref, grad_ref = refs[:3], refs[3:6], refs[6], refs[-2], refs[-1]
    b = pl.program_id(0)

    @pl.when(b == 0)
    def _():
        out_ref[...] = refs[7][...] if a else jnp.zeros_like(out_ref)
        grad_ref[...] = refs[8][...] if a else jnp.zeros_like(grad_ref)

    cells, channels = out_ref.shape
    d, h = v_refs[0].shape[0] - 2, v_refs[0].shape[1] - 2
    out, grad = out_ref[...], grad_ref[...]
    for c in range(3):
        k_hi, k_lo = split(k_ref[c])
        v_hi, v_lo = split(v_refs[c][a : a + d, pl.ds(b, h)].reshape(cells, channels))
        u_hi, u_lo = split(u_refs[2 - c][2 - a : 2 - a + d, pl.ds(2 - b, h)].reshape(cells, channels))
        for left, right in ((v_hi, k_hi), (v_hi, k_lo), (v_lo, k_hi)):
            out += jnp.dot(left, right, preferred_element_type=F32)
        for left, right in ((u_hi, k_hi), (u_hi, k_lo), (u_lo, k_hi)):
            grad += lax.dot_general(left, right, (((1,), (1,)), ((), ())), preferred_element_type=F32)
    out_ref[...] = out
    grad_ref[...] = grad


def shifted_3(padded):
    width = padded.shape[2] - 2
    return [padded[:, :, c : c + width] for c in range(3)]


def conv_third(a, windows, taps, before=()):
    planes, rows, width, channels = windows[0].shape
    cells = (planes - 2) * (rows - 2) * width
    whole = pl.BlockSpec((planes, rows, width, channels), lambda i: (0,) * 4)
    result = pl.BlockSpec((cells, channels), lambda i: (0, 0))
    shape = jax.ShapeDtypeStruct((cells, channels), F32)
    return pl.pallas_call(
        functools.partial(conv_kernel, a),
        grid=(3,),
        in_specs=[whole] * 6 + [pl.BlockSpec((3, channels, channels), lambda i: (3 * a + i, 0, 0))] + [result] * len(before),
        out_specs=[result, result],
        out_shape=[shape, shape],
        compiler_params=pltpu.CompilerParams(vmem_limit_bytes=40 * 2**20),
        cost_estimate=pl.CostEstimate(flops=2 * 6 * 9 * cells * channels * channels, bytes_accessed=4 * 2**20, transcendentals=0),
        name=f"conv_{a}",
    )(*windows, taps, *before)


def packed(two, h, w):
    lane = lax.broadcasted_iota(jnp.int32, (64, 128), 1)
    total = jnp.zeros((64, 128), F32)
    for i, x in enumerate(two):
        left, right = x[:, :128], x[:, 128:]
        for j, tile in enumerate((jnp.where(w == 0, left, right), jnp.where(w == 0, right, left))):
            turned = pltpu.roll(tile, lax.rem(32 * (2 * i + j) + 128 - 32 * h, 128), 1)
            total = jnp.where(lane // 32 == 2 * i + j, turned, total)
    return total


def messages_kernel(*refs):
    h, w = lax.axis_index("ha"), lax.axis_index("wa")
    v_ref, u_ref, out_refs = refs[0], refs[1], refs[2:]
    for k, out_ref in enumerate(out_refs):
        chip = lax.rem(h + k, 4)
        out_ref[0:256] = u_ref[...]
        for t in range(2):
            out_ref[256:320, 128 * t : 128 * t + 128] = packed((v_ref[2 * t], v_ref[2 * t + 1]), chip, w)


def ends_kernel(*refs):
    h, w = lax.axis_index("ha"), lax.axis_index("wa")
    below_ref, above_ref, out_refs = refs[0], refs[1], refs[2:]
    for k, out_ref in enumerate(out_refs):
        out_ref[...] = packed((below_ref[0], above_ref[0]), lax.rem(h + k, 4), w)


def for_chips(body, shape, *arrays):
    vmem = pl.BlockSpec(memory_space=pltpu.VMEM)
    return pl.pallas_call(
        body,
        out_shape=[jax.ShapeDtypeStruct(shape, F32)] * 4,
        in_specs=[vmem] * len(arrays),
        out_specs=[vmem] * 4,
        name=body.__name__,
    )(*arrays)


def lay_out(shifted, plane, first, second):
    lane = lax.broadcasted_iota(jnp.int32, (32, 8, 128), 2)
    row = lax.broadcasted_iota(jnp.int32, (32, 8, 128), 1)
    first = jnp.where(lane < 32, first, 0.0)
    second = jnp.where(lane < 32, second, 0.0)
    down_1, down_2 = pltpu.roll(first, 1, 1), pltpu.roll(second, 1, 1)
    up_1, up_2 = pltpu.roll(first, 7, 1), pltpu.roll(second, 7, 1)
    for w, (before, here, after) in enumerate(
        (
            (jnp.where(row == 0, down_2, down_1), first, jnp.where(row == 7, up_2, up_1)),
            (jnp.where(row == 0, down_1, down_2), second, jnp.where(row == 7, up_1, up_2)),
        )
    ):
        joined = before + pltpu.roll(here, 32, 2) + pltpu.roll(after, 64, 2)
        shifted[w, plane, pl.ds(1, 32)] = joined
        shifted[w, plane, 0] = joined[31]
        shifted[w, plane, 33] = joined[0]


def plane_of(refs, z, offset):
    tile = 128 * (z // 2)
    plane = jnp.concatenate([ref[256:320, tile : tile + 128].reshape(8, 8, 128) for ref in refs], axis=0)
    return pltpu.roll(plane, (128 - 64 * (z % 2) - offset) % 128, 2)


def plane_grad_kernel(scale, planes, pieces, *refs):
    mine, other = refs[:4], refs[4:8]
    out_refs, shifted, u_cat = refs[-2 - pieces : -2], refs[-2], refs[-1]
    share = out_refs[0].shape[0]
    for z in range(4):
        lay_out(shifted, z + 1, plane_of(mine, z, 0), plane_of(other, z, 32))
    if planes != (1,):
        own_halo, other_halo = (ref[...].reshape(32, 8, 128) for ref in refs[8:10])
        for i, z in enumerate((0, 5)):
            lay_out(shifted, z, pltpu.roll(own_halo, (128 - 64 * i) % 128, 2), pltpu.roll(other_halo, 96 - 64 * i, 2))
    for i, ref in enumerate(mine + other):
        hi, lo = split(ref[0:256].T)
        u_cat[i, :, 0:256] = hi
        u_cat[i, :, 256:512] = hi
        u_cat[i, :, 512:768] = lo
    windows = [(a, b) for a in planes for b in range(3)]
    for start in range(0, len(windows), 2):
        group = windows[start : start + 2]
        total = jnp.zeros((256, 128 * len(group)), F32)
        for w in range(2):
            for k in range(4):
                cells = [shifted[w, a : a + 4, 8 * k + b : 8 * k + b + 8].reshape(256, 128) for a, b in group]
                hi, lo = split(jnp.concatenate(cells, axis=1))
                right = jnp.concatenate([hi, lo, hi], axis=0)
                total += jnp.dot(u_cat[4 * w + k], right, preferred_element_type=F32)
        turned = total.T * scale
        for i in range(len(group)):
            for c in range(3):
                tap = 3 * (start + i) + c
                out_refs[tap // share][tap % share] = turned[128 * i + 32 * c : 128 * i + 32 * c + 32]


def plane_grad(scale, planes, pieces, messages, halo=()):
    vmem = pl.BlockSpec(memory_space=pltpu.VMEM)
    shapes = [jax.ShapeDtypeStruct((9 * len(planes) // pieces, 32, 256), F32)] * pieces
    return pl.pallas_call(
        functools.partial(plane_grad_kernel, scale, planes, pieces),
        out_shape=shapes,
        in_specs=[vmem] * (8 + len(halo)),
        out_specs=[vmem] * len(shapes),
        scratch_shapes=[pltpu.VMEM((2, 6, 34, 8, 128), F32), pltpu.VMEM((8, 256, 768), BF16)],
        compiler_params=pltpu.CompilerParams(vmem_limit_bytes=40 * 2**20),
        cost_estimate=pl.CostEstimate(flops=2 * 3 * 9 * len(planes) * 32 * 2048 * 256, bytes_accessed=4 * 2**20, transcendentals=0),
        name=f"plane_grad_{len(planes)}",
    )(*messages, *halo)


SWAP = [(0, 1), (1, 0)]
UP = [(i, (i + 1) % 4) for i in range(4)]
DOWN = [((i + 1) % 4, i) for i in range(4)]


def pair(bit):
    return [(i, i ^ bit) for i in range(4)]


INWARDS, MIDDLE, OUTWARDS = [(0, 1), (3, 2)], [(1, 2), (2, 1)], [(1, 0), (2, 3)]


def together(*arrays):
    return lax.optimization_barrier(arrays)


def to(x, axis, where):
    return lax.ppermute(x, axis, where)


def shared(volume, kernel, upstream):
    h, w = lax.axis_index("ha"), lax.axis_index("wa")
    channels = volume.shape[-1]
    taps = kernel.transpose(1, 0, 2)
    scale = 1.0 / math.sqrt(256 * 32)

    z = lax.axis_index("dev")
    end = (z == 0) | (z == 3)
    x_bit, y_bit = lax.rem(h, 2), h // 2

    def around(messages):
        return [messages[0]] + [to(messages[4 - k], "ha", [((i + k) % 4, i) for i in range(4)]) for k in (1, 2, 3)]

    mine = around(for_chips(messages_kernel, (320, channels), volume.reshape(4, 64, channels), upstream.reshape(256, channels)))
    other = [to(mine[0], "wa", SWAP)]

    volume, upstream, _ = together(volume, upstream, other[0])
    below = to(jnp.stack([volume[3], upstream[3]]), "dev", UP)
    above = to(jnp.stack([volume[0], upstream[0]]), "dev", DOWN)
    ends = for_chips(ends_kernel, (64, 128), below.reshape(2, 64, channels), above.reshape(2, 64, channels))
    *arrived, _ = together(*mine[1:], ends[0])
    mine = mine[:1] + arrived
    other += [to(x, "wa", SWAP) for x in arrived]
    own_halo = around(ends)
    *arrived, _ = together(*mine, *other, *own_halo)
    mine, other = arrived[:4], arrived[4:8]
    own_halo = jnp.stack(own_halo)
    other_halo = to(own_halo, "wa", SWAP)

    (a0,) = plane_grad(scale, (1,), 1, mine + other)
    a1 = to(a0, "dev", INWARDS)
    b0, c0 = plane_grad(scale, (0, 2), 2, mine + other, (own_halo, other_halo))
    b1, c1 = to(b0, "dev", INWARDS), to(c0, "dev", INWARDS)
    a0, _ = together(a0 + a1, b0)
    a1 = to(a0, "dev", MIDDLE)

    def edge(row):
        return jnp.concatenate([below[:, row : row + 1], volume[:, row : row + 1], above[:, row : row + 1]], axis=0)

    low_edge, high_edge, _ = together(edge(0), edge(7), c0)
    behind, ahead = to(high_edge, "ha", UP), to(low_edge, "ha", DOWN)
    a1, b1, behind, ahead = together(a1, b1, behind, ahead)
    a0, b0 = a0 + a1, b0 + b1

    a1, b1 = to(a0, "dev", OUTWARDS), to(b0, "dev", MIDDLE)
    deep = jnp.concatenate([below, volume, above], axis=0)
    rows = jnp.concatenate([behind, deep, ahead], axis=1)
    v_rows = jnp.concatenate([rows[0:1], rows[2:7]], axis=0)
    u_own = [x[:256].reshape(4, 8, 8, channels) for x in mine]
    u_rows = jnp.concatenate([u_own[3][:, 7:8], u_own[0], u_own[1][:, 0:1]], axis=1)
    u_rows = jnp.concatenate([rows[1:2], u_rows, rows[7:8]], axis=0)
    both = jnp.concatenate([v_rows, u_rows], axis=0)
    sides = to(jnp.concatenate([both[:, :, 7:8], both[:, :, 0:1]], axis=2), "wa", SWAP)
    both = jnp.concatenate([sides[:, :, 0:1], both, sides[:, :, 1:2]], axis=2)
    windows = shifted_3(both[:6]) + shifted_3(both[6:])
    a1, b1, c1, *windows = together(a1, b1, c1, *windows)
    a0, b0, c0 = jnp.where(end, a1, a0), b0 + b1, c0 + c1

    def first_half(x):
        return to(x[:5], "ha", pair(1)), to(x[5:], "ha", pair(2))

    def joined(x, got):
        along_x, along_y = ([x[:5], got[0]], 2, x_bit), ([x[5:], got[1]], 1, y_bit)
        both = []
        for (own, other), axis, bit in (along_x, along_y):
            own, other = (jnp.expand_dims(t, (1, 2)) for t in (own, other))
            both.append(jnp.where(bit == 0, jnp.concatenate([own, other], axis), jnp.concatenate([other, own], axis)))
        return both

    def second_half(x):
        return to(x[0], "ha", pair(2)), to(x[1], "ha", pair(1))

    def placed(total, tap, x, far):
        for part, y in ((x[0], y_bit), (far[0], 1 - y_bit)):
            total = lax.dynamic_update_slice(total, part, (tap, y, 0, 0, 0))
        for part, x in ((x[1], x_bit), (far[1], 1 - x_bit)):
            total = lax.dynamic_update_slice(total, part, (tap + 5, 0, x, 0, 0))
        return total

    conv = conv_third(0, windows, taps)
    a_got = first_half(a0)
    a0, a1, a2, b1, c1, *conv = together(a0, *a_got, to(b0, "dev", OUTWARDS), to(c0, "dev", MIDDLE), *conv)
    b0, c0, a0 = jnp.where(end, b1, b0), c0 + c1, joined(a0, (a1, a2))

    a_far = second_half(a0)
    conv = conv_third(1, windows, taps, conv)
    b_got = first_half(b0)
    b0, b1, b2, c1, *conv = together(b0, *b_got, to(c0, "dev", OUTWARDS), *conv)
    c0, b0 = jnp.where(end, c1, c0), joined(b0, (b1, b2))

    b_far = second_half(b0)
    conv = conv_third(2, windows, taps, conv)
    c_got = first_half(c0)
    c0, c1, c2, *conv = together(c0, *c_got, *conv)
    c0 = joined(c0, (c1, c2))
    c_far = second_half(c0)

    kernel_grad = jnp.zeros((27, 2, 2, 32, channels), F32)
    kernel_grad = placed(kernel_grad, 9, a0, a_far)
    kernel_grad = placed(kernel_grad, 0, b0, b_far)
    kernel_grad = placed(kernel_grad, 18, c0, c_far)
    output, volume_grad = conv
    return output.reshape(volume.shape), volume_grad.reshape(volume.shape), kernel_grad.reshape(27, 128, channels).transpose(1, 0, 2)


def solution(mesh):
    sizes = tuple(mesh.shape[name] for name in ("dev", "ha", "wa"))
    placed = (P("dev", "ha", "wa", None), P(), P("dev", "ha", "wa", None))

    def per_device(volume, kernel, upstream):
        fits = sizes == (4, 4, 2) and volume.shape == (4, 8, 8, 256) and kernel.shape == (256, 27, 256)
        return (shared if fits else plain)(volume, kernel, upstream)

    return jax.shard_map(
        per_device,
        mesh=mesh,
        in_specs=placed,
        out_specs=(P("dev", "ha", "wa", None), P("dev", "ha", "wa", None), P("wa", None, None)),
        check_vma=False,
    )
```

```python
import functools
import math

import jax
import jax.numpy as jnp
from jax import lax
from jax.experimental import pallas as pl
from jax.experimental.pallas import tpu as pltpu
from jax.sharding import PartitionSpec as P

F32, BF16 = jnp.float32, jnp.bfloat16


def split(x):
    hi = x.astype(BF16)
    return hi, (x - hi.astype(F32)).astype(BF16)


def padded_by_halo(shard, sides):
    for axis, dim in sides:
        count, length = lax.axis_size(axis), shard.shape[dim]
        up = [(i, (i + 1) % count) for i in range(count)]
        down = [(j, i) for i, j in up]
        before = lax.ppermute(lax.slice_in_dim(shard, length - 1, length, axis=dim), axis, up)
        after = lax.ppermute(lax.slice_in_dim(shard, 0, 1, axis=dim), axis, down)
        shard = jnp.concatenate([before, shard, after], axis=dim)
    return shard


def plain(volume, kernel, upstream):
    depth, height, width, channels = volume.shape
    cells = depth * height * width
    padded = padded_by_halo(jnp.stack([volume, upstream]), (("dev", 1), ("ha", 2), ("wa", 3)))

    def windows(which, sign):
        return jnp.stack(
            [
                padded[which, 1 + sign * a :, 1 + sign * b :, 1 + sign * c :][:depth, :height, :width].reshape(cells, channels)
                for a in (-1, 0, 1) for b in (-1, 0, 1) for c in (-1, 0, 1)
            ],
            axis=1,
        )

    dot = functools.partial(jnp.einsum, precision=lax.Precision.HIGHEST, preferred_element_type=F32)
    forward, backward = windows(0, 1), windows(1, -1)
    output = dot("ntc,cto->no", forward, kernel)
    volume_grad = dot("nto,cto->nc", backward, kernel)
    total = cells * lax.axis_size("dev") * lax.axis_size("ha") * lax.axis_size("wa")
    summed = lax.psum(dot("ntc,no->cto", forward, upstream.reshape(cells, channels)) * (1.0 / math.sqrt(total)), ("dev", "ha", "wa"))
    owned = channels // lax.axis_size("wa")
    kernel_grad = lax.dynamic_slice_in_dim(summed, lax.axis_index("wa") * owned, owned, 0)
    return output.reshape(volume.shape), volume_grad.reshape(volume.shape), kernel_grad


def conv_kernel(a, *refs):
    v_refs, u_refs, k_ref, out_ref, grad_ref = refs[:3], refs[3:6], refs[6], refs[-2], refs[-1]
    b = pl.program_id(0)

    @pl.when(b == 0)
    def _():
        out_ref[...] = refs[7][...] if a else jnp.zeros_like(out_ref)
        grad_ref[...] = refs[8][...] if a else jnp.zeros_like(grad_ref)

    cells, channels = out_ref.shape
    d, h = v_refs[0].shape[0] - 2, v_refs[0].shape[1] - 2
    out, grad = out_ref[...], grad_ref[...]
    for c in range(3):
        k_hi, k_lo = split(k_ref[c])
        v_hi, v_lo = split(v_refs[c][a : a + d, pl.ds(b, h)].reshape(cells, channels))
        u_hi, u_lo = split(u_refs[2 - c][2 - a : 2 - a + d, pl.ds(2 - b, h)].reshape(cells, channels))
        for left, right in ((v_hi, k_hi), (v_hi, k_lo), (v_lo, k_hi)):
            out += jnp.dot(left, right, preferred_element_type=F32)
        for left, right in ((u_hi, k_hi), (u_hi, k_lo), (u_lo, k_hi)):
            grad += lax.dot_general(left, right, (((1,), (1,)), ((), ())), preferred_element_type=F32)
    out_ref[...] = out
    grad_ref[...] = grad


def shifted_3(padded):
    width = padded.shape[2] - 2
    return [padded[:, :, c : c + width] for c in range(3)]


def conv_third(a, windows, taps, before=()):
    planes, rows, width, channels = windows[0].shape
    cells = (planes - 2) * (rows - 2) * width
    whole = pl.BlockSpec((planes, rows, width, channels), lambda i: (0,) * 4)
    result = pl.BlockSpec((cells, channels), lambda i: (0, 0))
    shape = jax.ShapeDtypeStruct((cells, channels), F32)
    return pl.pallas_call(
        functools.partial(conv_kernel, a),
        grid=(3,),
        in_specs=[whole] * 6 + [pl.BlockSpec((3, channels, channels), lambda i: (3 * a + i, 0, 0))] + [result] * len(before),
        out_specs=[result, result],
        out_shape=[shape, shape],
        compiler_params=pltpu.CompilerParams(vmem_limit_bytes=40 * 2**20),
        cost_estimate=pl.CostEstimate(flops=2 * 6 * 9 * cells * channels * channels, bytes_accessed=4 * 2**20, transcendentals=0),
        name=f"conv_{a}",
    )(*windows, taps, *before)


def packed(two, h, w):
    lane = lax.broadcasted_iota(jnp.int32, (64, 128), 1)
    total = jnp.zeros((64, 128), F32)
    for i, x in enumerate(two):
        left, right = x[:, :128], x[:, 128:]
        for j, tile in enumerate((jnp.where(w == 0, left, right), jnp.where(w == 0, right, left))):
            turned = pltpu.roll(tile, lax.rem(32 * (2 * i + j) + 128 - 32 * h, 128), 1)
            total = jnp.where(lane // 32 == 2 * i + j, turned, total)
    return total


def messages_kernel(below_ref, volume_ref, above_ref, *out_refs):
    h, w = lax.axis_index("ha"), lax.axis_index("wa")
    planes = [below_ref[0], *(volume_ref[z] for z in range(4)), above_ref[0]]
    for k, out_ref in enumerate(out_refs):
        for t in range(3):
            out_ref[:, 128 * t : 128 * t + 128] = packed(planes[2 * t : 2 * t + 2], lax.rem(h + k, 4), w)


def messages(below, volume, above):
    vmem = pl.BlockSpec(memory_space=pltpu.VMEM)
    return pl.pallas_call(
        messages_kernel,
        out_shape=[jax.ShapeDtypeStruct((64, 384), F32)] * 4,
        in_specs=[vmem] * 3,
        out_specs=[vmem] * 4,
        name="messages",
    )(below, volume, above)


def lay_out(shifted, plane, first, second):
    lane = lax.broadcasted_iota(jnp.int32, (32, 8, 128), 2)
    row = lax.broadcasted_iota(jnp.int32, (32, 8, 128), 1)
    first = jnp.where(lane < 32, first, 0.0)
    second = jnp.where(lane < 32, second, 0.0)
    down_1, down_2 = pltpu.roll(first, 1, 1), pltpu.roll(second, 1, 1)
    up_1, up_2 = pltpu.roll(first, 7, 1), pltpu.roll(second, 7, 1)
    for w, (before, here, after) in enumerate(
        (
            (jnp.where(row == 0, down_2, down_1), first, jnp.where(row == 7, up_2, up_1)),
            (jnp.where(row == 0, down_1, down_2), second, jnp.where(row == 7, up_1, up_2)),
        )
    ):
        joined = before + pltpu.roll(here, 32, 2) + pltpu.roll(after, 64, 2)
        shifted[w, plane, pl.ds(1, 32)] = joined
        shifted[w, plane, 0] = joined[31]
        shifted[w, plane, 33] = joined[0]


def plane_of(refs, z, offset):
    tile = 128 * (z // 2)
    plane = jnp.concatenate([ref[:, tile : tile + 128].reshape(8, 8, 128) for ref in refs], axis=0)
    return pltpu.roll(plane, (128 - 64 * (z % 2) - offset) % 128, 2)


def plane_grad_kernel(scale, planes, *refs):
    u_refs, mine, other, out_refs, shifted, u_cat = refs[:8], refs[8:12], refs[12:16], refs[16:-2], refs[-2], refs[-1]
    share = out_refs[0].shape[0]
    for z in range(1, 5) if planes == (1,) else range(6):
        lay_out(shifted, z, plane_of(mine, z, 0), plane_of(other, z, 32))
    for i, ref in enumerate(u_refs):
        hi, lo = split(ref[...].T)
        u_cat[i, :, 0:256] = hi
        u_cat[i, :, 256:512] = hi
        u_cat[i, :, 512:768] = lo
    windows = [(a, b) for a in planes for b in range(3)]
    for start in range(0, len(windows), 2):
        group = windows[start : start + 2]
        total = jnp.zeros((256, 128 * len(group)), F32)
        for w in range(2):
            for k in range(4):
                cells = [shifted[w, a : a + 4, 8 * k + b : 8 * k + b + 8].reshape(256, 128) for a, b in group]
                hi, lo = split(jnp.concatenate(cells, axis=1))
                right = jnp.concatenate([hi, lo, hi], axis=0)
                total += jnp.dot(u_cat[4 * w + k], right, preferred_element_type=F32)
        turned = total.T * scale
        for i in range(len(group)):
            for c in range(3):
                tap = 3 * (start + i) + c
                out_refs[tap // share][tap % share] = turned[128 * i + 32 * c : 128 * i + 32 * c + 32]


def plane_grad(scale, planes, pieces, blocks):
    vmem = pl.BlockSpec(memory_space=pltpu.VMEM)
    return pl.pallas_call(
        functools.partial(plane_grad_kernel, scale, planes),
        out_shape=[jax.ShapeDtypeStruct((9 * len(planes) // pieces, 32, 256), F32)] * pieces,
        in_specs=[vmem] * 16,
        out_specs=[vmem] * pieces,
        scratch_shapes=[pltpu.VMEM((2, 6, 34, 8, 128), F32), pltpu.VMEM((8, 256, 768), BF16)],
        compiler_params=pltpu.CompilerParams(vmem_limit_bytes=40 * 2**20),
        cost_estimate=pl.CostEstimate(flops=2 * 3 * 9 * len(planes) * 32 * 2048 * 256, bytes_accessed=4 * 2**20, transcendentals=0),
        name=f"plane_grad_{len(planes)}",
    )(*blocks)


SWAP = [(0, 1), (1, 0)]
UP = [(i, (i + 1) % 4) for i in range(4)]
DOWN = [((i + 1) % 4, i) for i in range(4)]


def pair(bit):
    return [(i, i ^ bit) for i in range(4)]


INWARDS, MIDDLE, OUTWARDS = [(0, 1), (3, 2)], [(1, 2), (2, 1)], [(1, 0), (2, 3)]


def together(*arrays):
    return lax.optimization_barrier(arrays)


def to(x, axis, where):
    return lax.ppermute(x, axis, where)


def shared(volume, kernel, upstream):
    h, w = lax.axis_index("ha"), lax.axis_index("wa")
    channels = volume.shape[-1]
    taps = kernel.transpose(1, 0, 2)
    scale = 1.0 / math.sqrt(256 * 32)

    z = lax.axis_index("dev")
    end = (z == 0) | (z == 3)
    x_bit, y_bit = lax.rem(h, 2), h // 2

    def around(messages):
        return [messages[0]] + [to(messages[4 - k], "ha", [((i + k) % 4, i) for i in range(4)]) for k in (1, 2, 3)]

    u_mine = around([upstream.reshape(256, channels)] * 4)
    u_other = [to(u_mine[0], "wa", SWAP)]
    volume, upstream, _ = together(volume, upstream, u_other[0])
    below = to(jnp.stack([volume[3], upstream[3]]), "dev", UP)
    above = to(jnp.stack([volume[0], upstream[0]]), "dev", DOWN)
    parts = messages(below.reshape(2, 64, channels), volume.reshape(4, 64, channels), above.reshape(2, 64, channels))
    v_mine = around(parts)
    *arrived, _ = together(*u_mine[1:], parts[0])
    u_mine = u_mine[:1] + arrived
    u_other += [to(x, "wa", SWAP) for x in arrived]
    v_other = [to(x, "wa", SWAP) for x in v_mine]
    blocks = together(*u_mine, *u_other, *v_mine, *v_other)

    (a0,) = plane_grad(scale, (1,), 1, blocks)

    def edge(row):
        return jnp.concatenate([below[:, row : row + 1], volume[:, row : row + 1], above[:, row : row + 1]], axis=0)

    low_edge, high_edge, _ = together(edge(0), edge(7), a0)
    behind, ahead = to(high_edge, "ha", UP), to(low_edge, "ha", DOWN)
    a1 = to(a0, "dev", INWARDS)
    b0, c0 = plane_grad(scale, (0, 2), 2, blocks)
    b1, c1 = to(b0, "dev", INWARDS), to(c0, "dev", INWARDS)
    a0, behind, ahead, _ = together(a0 + a1, behind, ahead, b0)
    a1 = to(a0, "dev", MIDDLE)
    a1, b1 = together(a1, b1)
    a0, b0 = a0 + a1, b0 + b1

    a1, b1 = to(a0, "dev", OUTWARDS), to(b0, "dev", MIDDLE)
    deep = jnp.concatenate([below, volume, above], axis=0)
    rows = jnp.concatenate([behind, deep, ahead], axis=1)
    v_rows = jnp.concatenate([rows[0:1], rows[2:7]], axis=0)
    u_own = [x.reshape(4, 8, 8, channels) for x in u_mine]
    u_rows = jnp.concatenate([u_own[3][:, 7:8], u_own[0], u_own[1][:, 0:1]], axis=1)
    u_rows = jnp.concatenate([rows[1:2], u_rows, rows[7:8]], axis=0)
    both = jnp.concatenate([v_rows, u_rows], axis=0)
    sides = to(jnp.concatenate([both[:, :, 7:8], both[:, :, 0:1]], axis=2), "wa", SWAP)
    both = jnp.concatenate([sides[:, :, 0:1], both, sides[:, :, 1:2]], axis=2)
    windows = shifted_3(both[:6]) + shifted_3(both[6:])
    a1, b1, c1, *windows = together(a1, b1, c1, *windows)
    a0, b0, c0 = jnp.where(end, a1, a0), b0 + b1, c0 + c1

    def first_half(x):
        return to(x[:5], "ha", pair(1)), to(x[5:], "ha", pair(2))

    def joined(x, got):
        along_x, along_y = ([x[:5], got[0]], 2, x_bit), ([x[5:], got[1]], 1, y_bit)
        both = []
        for (own, other), axis, bit in (along_x, along_y):
            own, other = (jnp.expand_dims(t, (1, 2)) for t in (own, other))
            both.append(jnp.where(bit == 0, jnp.concatenate([own, other], axis), jnp.concatenate([other, own], axis)))
        return both

    def second_half(x):
        return to(x[0], "ha", pair(2)), to(x[1], "ha", pair(1))

    def placed(total, tap, x, far):
        for part, y in ((x[0], y_bit), (far[0], 1 - y_bit)):
            total = lax.dynamic_update_slice(total, part, (tap, y, 0, 0, 0))
        for part, x in ((x[1], x_bit), (far[1], 1 - x_bit)):
            total = lax.dynamic_update_slice(total, part, (tap + 5, 0, x, 0, 0))
        return total

    conv = conv_third(0, windows, taps)
    a_got = first_half(a0)
    a0, a1, a2, b1, c1, *conv = together(a0, *a_got, to(b0, "dev", OUTWARDS), to(c0, "dev", MIDDLE), *conv)
    b0, c0, a0 = jnp.where(end, b1, b0), c0 + c1, joined(a0, (a1, a2))

    a_far = second_half(a0)
    conv = conv_third(1, windows, taps, conv)
    b_got = first_half(b0)
    b0, b1, b2, c1, *rest = together(b0, *b_got, to(c0, "dev", OUTWARDS), *a_far, *conv)
    a_far, conv = rest[:2], rest[2:]
    c0, b0 = jnp.where(end, c1, c0), joined(b0, (b1, b2))

    b_far = second_half(b0)
    conv = conv_third(2, windows, taps, conv)
    c_got = first_half(c0)
    c0, c1, c2, *rest = together(c0, *c_got, *b_far, *conv)
    b_far, conv = rest[:2], rest[2:]
    c0 = joined(c0, (c1, c2))
    c_far = together(*second_half(c0))

    kernel_grad = jnp.zeros((27, 2, 2, 32, channels), F32)
    kernel_grad = placed(kernel_grad, 9, a0, a_far)
    kernel_grad = placed(kernel_grad, 0, b0, b_far)
    kernel_grad = placed(kernel_grad, 18, c0, c_far)
    output, volume_grad = conv
    return output.reshape(volume.shape), volume_grad.reshape(volume.shape), kernel_grad.reshape(27, 128, channels).transpose(1, 0, 2)


def solution(mesh):
    sizes = tuple(mesh.shape[name] for name in ("dev", "ha", "wa"))
    placed = (P("dev", "ha", "wa", None), P(), P("dev", "ha", "wa", None))

    def per_device(volume, kernel, upstream):
        fits = sizes == (4, 4, 2) and volume.shape == (4, 8, 8, 256) and kernel.shape == (256, 27, 256)
        return (shared if fits else plain)(volume, kernel, upstream)

    return jax.shard_map(
        per_device,
        mesh=mesh,
        in_specs=placed,
        out_specs=(P("dev", "ha", "wa", None), P("dev", "ha", "wa", None), P("wa", None, None)),
        check_vma=False,
    )
```

```python
import functools
import math

import jax
import jax.numpy as jnp
from jax import lax
from jax.experimental import pallas as pl
from jax.experimental.pallas import tpu as pltpu
from jax.sharding import PartitionSpec as P

F32, BF16 = jnp.float32, jnp.bfloat16


def split(x):
    hi = x.astype(BF16)
    return hi, (x - hi.astype(F32)).astype(BF16)


def padded_by_halo(shard, sides):
    for axis, dim in sides:
        count, length = lax.axis_size(axis), shard.shape[dim]
        up = [(i, (i + 1) % count) for i in range(count)]
        down = [(j, i) for i, j in up]
        before = lax.ppermute(lax.slice_in_dim(shard, length - 1, length, axis=dim), axis, up)
        after = lax.ppermute(lax.slice_in_dim(shard, 0, 1, axis=dim), axis, down)
        shard = jnp.concatenate([before, shard, after], axis=dim)
    return shard


def plain(volume, kernel, upstream):
    depth, height, width, channels = volume.shape
    cells = depth * height * width
    padded = padded_by_halo(jnp.stack([volume, upstream]), (("dev", 1), ("ha", 2), ("wa", 3)))

    def windows(which, sign):
        return jnp.stack(
            [
                padded[which, 1 + sign * a :, 1 + sign * b :, 1 + sign * c :][:depth, :height, :width].reshape(cells, channels)
                for a in (-1, 0, 1) for b in (-1, 0, 1) for c in (-1, 0, 1)
            ],
            axis=1,
        )

    dot = functools.partial(jnp.einsum, precision=lax.Precision.HIGHEST, preferred_element_type=F32)
    forward, backward = windows(0, 1), windows(1, -1)
    output = dot("ntc,cto->no", forward, kernel)
    volume_grad = dot("nto,cto->nc", backward, kernel)
    total = cells * lax.axis_size("dev") * lax.axis_size("ha") * lax.axis_size("wa")
    summed = lax.psum(dot("ntc,no->cto", forward, upstream.reshape(cells, channels)) * (1.0 / math.sqrt(total)), ("dev", "ha", "wa"))
    owned = channels // lax.axis_size("wa")
    kernel_grad = lax.dynamic_slice_in_dim(summed, lax.axis_index("wa") * owned, owned, 0)
    return output.reshape(volume.shape), volume_grad.reshape(volume.shape), kernel_grad


def conv_kernel(a, *refs):
    v_refs, u_refs, k_ref, out_ref, grad_ref = refs[:3], refs[3:6], refs[6], refs[-2], refs[-1]
    b = pl.program_id(0)

    @pl.when(b == 0)
    def _():
        out_ref[...] = refs[7][...] if a else jnp.zeros_like(out_ref)
        grad_ref[...] = refs[8][...] if a else jnp.zeros_like(grad_ref)

    cells, channels = out_ref.shape
    d, h = v_refs[0].shape[0] - 2, v_refs[0].shape[1] - 2
    out, grad = out_ref[...], grad_ref[...]
    for c in range(3):
        k_hi, k_lo = split(k_ref[c])
        v_hi, v_lo = split(v_refs[c][a : a + d, pl.ds(b, h)].reshape(cells, channels))
        u_hi, u_lo = split(u_refs[2 - c][2 - a : 2 - a + d, pl.ds(2 - b, h)].reshape(cells, channels))
        for left, right in ((v_hi, k_hi), (v_hi, k_lo), (v_lo, k_hi)):
            out += jnp.dot(left, right, preferred_element_type=F32)
        for left, right in ((u_hi, k_hi), (u_hi, k_lo), (u_lo, k_hi)):
            grad += lax.dot_general(left, right, (((1,), (1,)), ((), ())), preferred_element_type=F32)
    out_ref[...] = out
    grad_ref[...] = grad


def shifted_3(padded):
    width = padded.shape[2] - 2
    return [padded[:, :, c : c + width] for c in range(3)]


def conv_third(a, windows, taps, before=()):
    planes, rows, width, channels = windows[0].shape
    cells = (planes - 2) * (rows - 2) * width
    whole = pl.BlockSpec((planes, rows, width, channels), lambda i: (0,) * 4)
    result = pl.BlockSpec((cells, channels), lambda i: (0, 0))
    shape = jax.ShapeDtypeStruct((cells, channels), F32)
    return pl.pallas_call(
        functools.partial(conv_kernel, a),
        grid=(3,),
        in_specs=[whole] * 6 + [pl.BlockSpec((3, channels, channels), lambda i: (3 * a + i, 0, 0))] + [result] * len(before),
        out_specs=[result, result],
        out_shape=[shape, shape],
        compiler_params=pltpu.CompilerParams(vmem_limit_bytes=40 * 2**20),
        cost_estimate=pl.CostEstimate(flops=2 * 6 * 9 * cells * channels * channels, bytes_accessed=4 * 2**20, transcendentals=0),
        name=f"conv_{a}",
    )(*windows, taps, *before)


def messages_kernel(below_ref, volume_ref, above_ref, *out_refs):
    h, w = lax.axis_index("ha"), lax.axis_index("wa")
    lane = lax.broadcasted_iota(jnp.int32, (64, 128), 1) // 32
    for t in range(3):
        tiles = []
        for z in (2 * t, 2 * t + 1):
            x = below_ref[0] if z == 0 else above_ref[0] if z == 5 else volume_ref[z - 1]
            left, right = x[:, :128], x[:, 128:]
            for tile in (jnp.where(w == 0, left, right), jnp.where(w == 0, right, left)):
                tiles.append(pltpu.roll(tile, lax.rem(128 - 32 * h, 128), 1))
        for k, out_ref in enumerate(out_refs):
            total = tiles[0] if k == 0 else pltpu.roll(tiles[0], 128 - 32 * k, 1)
            for j in range(1, 4):
                shift = 32 * (j - k) % 128
                total = jnp.where(lane == j, pltpu.roll(tiles[j], shift, 1) if shift else tiles[j], total)
            out_ref[:, 128 * t : 128 * t + 128] = total


def messages(below, volume, above):
    vmem = pl.BlockSpec(memory_space=pltpu.VMEM)
    return pl.pallas_call(
        messages_kernel,
        out_shape=[jax.ShapeDtypeStruct((64, 384), F32)] * 4,
        in_specs=[vmem] * 3,
        out_specs=[vmem] * 4,
        compiler_params=pltpu.CompilerParams(vmem_limit_bytes=4 * 2**20),
        name="messages",
    )(below, volume, above)


def lay_out(shifted, plane, first, second):
    lane = lax.broadcasted_iota(jnp.int32, (32, 8, 128), 2)
    row = lax.broadcasted_iota(jnp.int32, (32, 8, 128), 1)
    first = jnp.where(lane < 32, first, 0.0)
    second = jnp.where(lane < 32, second, 0.0)
    down_1, down_2 = pltpu.roll(first, 1, 1), pltpu.roll(second, 1, 1)
    up_1, up_2 = pltpu.roll(first, 7, 1), pltpu.roll(second, 7, 1)
    for w, (before, here, after) in enumerate(
        (
            (jnp.where(row == 0, down_2, down_1), first, jnp.where(row == 7, up_2, up_1)),
            (jnp.where(row == 0, down_1, down_2), second, jnp.where(row == 7, up_1, up_2)),
        )
    ):
        joined = before + pltpu.roll(here, 32, 2) + pltpu.roll(after, 64, 2)
        shifted[w, plane, pl.ds(1, 32)] = joined
        shifted[w, plane, 0] = joined[31]
        shifted[w, plane, 33] = joined[0]


def plane_of(refs, z, offset):
    tile = 128 * (z // 2)
    plane = jnp.concatenate([ref[:, tile : tile + 128].reshape(8, 8, 128) for ref in refs], axis=0)
    return pltpu.roll(plane, (128 - 64 * (z % 2) - offset) % 128, 2)


def plane_grad_kernel(scale, planes, *refs):
    u_refs, mine, other, out_refs, shifted, u_cat = refs[:8], refs[8:12], refs[12:16], refs[16:-2], refs[-2], refs[-1]
    share = out_refs[0].shape[0]
    for z in range(1, 5) if planes == (1,) else range(6):
        lay_out(shifted, z, plane_of(mine, z, 0), plane_of(other, z, 32))
    for i, ref in enumerate(u_refs):
        hi, lo = split(ref[...].T)
        u_cat[i, :, 0:256] = hi
        u_cat[i, :, 256:512] = hi
        u_cat[i, :, 512:768] = lo
    windows = [(a, b) for a in planes for b in range(3)]
    for start in range(0, len(windows), 2):
        group = windows[start : start + 2]
        total = jnp.zeros((256, 128 * len(group)), F32)
        for w in range(2):
            for k in range(4):
                cells = [shifted[w, a : a + 4, 8 * k + b : 8 * k + b + 8].reshape(256, 128) for a, b in group]
                hi, lo = split(jnp.concatenate(cells, axis=1))
                right = jnp.concatenate([hi, lo, hi], axis=0)
                total += jnp.dot(u_cat[4 * w + k], right, preferred_element_type=F32)
        turned = total.T * scale
        for i in range(len(group)):
            for c in range(3):
                tap = 3 * (start + i) + c
                out_refs[tap // share][tap % share] = turned[128 * i + 32 * c : 128 * i + 32 * c + 32]


def plane_grad(scale, planes, pieces, blocks):
    vmem = pl.BlockSpec(memory_space=pltpu.VMEM)
    return pl.pallas_call(
        functools.partial(plane_grad_kernel, scale, planes),
        out_shape=[jax.ShapeDtypeStruct((9 * len(planes) // pieces, 32, 256), F32)] * pieces,
        in_specs=[vmem] * 16,
        out_specs=[vmem] * pieces,
        scratch_shapes=[pltpu.VMEM((2, 6, 34, 8, 128), F32), pltpu.VMEM((8, 256, 768), BF16)],
        compiler_params=pltpu.CompilerParams(vmem_limit_bytes=40 * 2**20),
        cost_estimate=pl.CostEstimate(flops=2 * 3 * 9 * len(planes) * 32 * 2048 * 256, bytes_accessed=4 * 2**20, transcendentals=0),
        name=f"plane_grad_{len(planes)}",
    )(*blocks)


SWAP = [(0, 1), (1, 0)]
UP = [(i, (i + 1) % 4) for i in range(4)]
DOWN = [((i + 1) % 4, i) for i in range(4)]


def pair(bit):
    return [(i, i ^ bit) for i in range(4)]


INWARDS, MIDDLE, OUTWARDS = [(0, 1), (3, 2)], [(1, 2), (2, 1)], [(1, 0), (2, 3)]


def together(*arrays):
    return lax.optimization_barrier(arrays)


def to(x, axis, where):
    return lax.ppermute(x, axis, where)


def shared(volume, kernel, upstream):
    h, w = lax.axis_index("ha"), lax.axis_index("wa")
    channels = volume.shape[-1]
    taps = kernel.transpose(1, 0, 2)
    scale = 1.0 / math.sqrt(256 * 32)

    z = lax.axis_index("dev")
    end = (z == 0) | (z == 3)
    x_bit, y_bit = lax.rem(h, 2), h // 2

    def around(messages):
        return [messages[0]] + [to(messages[4 - k], "ha", [((i + k) % 4, i) for i in range(4)]) for k in (1, 2, 3)]

    u_mine = around([upstream.reshape(256, channels)] * 4)
    u_other = [to(u_mine[0], "wa", SWAP)]
    volume, upstream, u_other[0] = together(volume, upstream, u_other[0])
    below = to(jnp.stack([volume[3], upstream[3]]), "dev", UP)
    above = to(jnp.stack([volume[0], upstream[0]]), "dev", DOWN)
    parts = messages(below.reshape(2, 64, channels), volume.reshape(4, 64, channels), above.reshape(2, 64, channels))
    v_mine = around(parts)
    *arrived, _ = together(*u_mine[1:], parts[0])
    u_mine = u_mine[:1] + arrived
    u_other += [to(x, "wa", SWAP) for x in arrived]
    v_other = [to(x, "wa", SWAP) for x in v_mine]
    blocks = [*u_mine, *u_other, *v_mine, *v_other]

    (a0,) = plane_grad(scale, (1,), 1, blocks)

    a1 = to(a0, "dev", INWARDS)
    b0, c0 = plane_grad(scale, (0, 2), 2, blocks)
    b1, c1 = to(b0, "dev", INWARDS), to(c0, "dev", INWARDS)
    a0, b0 = together(a0 + a1, b0)
    a1 = to(a0, "dev", MIDDLE)
    a1, b1 = together(a1, b1)
    a0, b0 = a0 + a1, b0 + b1

    def edge(row):
        return jnp.concatenate([below[:, row : row + 1], volume[:, row : row + 1], above[:, row : row + 1]], axis=0)

    low_edge, high_edge, b0 = together(edge(0), edge(7), b0)
    behind, ahead = to(high_edge, "ha", UP), to(low_edge, "ha", DOWN)
    a1, b1 = to(a0, "dev", OUTWARDS), to(b0, "dev", MIDDLE)
    a1, b1, c1, behind, ahead = together(a1, b1, c1, behind, ahead)
    a0, b0, c0 = jnp.where(end, a1, a0), b0 + b1, c0 + c1
    deep = jnp.concatenate([below, volume, above], axis=0)
    rows = jnp.concatenate([behind, deep, ahead], axis=1)
    v_rows = jnp.concatenate([rows[0:1], rows[2:7]], axis=0)
    u_own = [x.reshape(4, 8, 8, channels) for x in u_mine]
    u_rows = jnp.concatenate([u_own[3][:, 7:8], u_own[0], u_own[1][:, 0:1]], axis=1)
    u_rows = jnp.concatenate([rows[1:2], u_rows, rows[7:8]], axis=0)
    both = jnp.concatenate([v_rows, u_rows], axis=0)
    sides = to(jnp.concatenate([both[:, :, 7:8], both[:, :, 0:1]], axis=2), "wa", SWAP)
    both = jnp.concatenate([sides[:, :, 0:1], both, sides[:, :, 1:2]], axis=2)
    windows = shifted_3(both[:6]) + shifted_3(both[6:])

    def first_half(x):
        return to(x[:, :16], "ha", pair(1)), to(x[:, 16:], "ha", pair(2))

    def joined(x, got):
        along_x, along_y = ([x[:, :16], got[0]], 2, x_bit), ([x[:, 16:], got[1]], 1, y_bit)
        both = []
        for (own, other), axis, bit in (along_x, along_y):
            own, other = (jnp.expand_dims(t, (1, 2)) for t in (own, other))
            both.append(jnp.where(bit == 0, jnp.concatenate([own, other], axis), jnp.concatenate([other, own], axis)))
        return both

    def second_half(x):
        return to(x[0], "ha", pair(2)), to(x[1], "ha", pair(1))

    def placed(total, tap, x, far):
        for part, y in ((x[0], y_bit), (far[0], 1 - y_bit)):
            total = lax.dynamic_update_slice(total, part, (tap, y, 0, 0, 0))
        for part, x in ((x[1], x_bit), (far[1], 1 - x_bit)):
            total = lax.dynamic_update_slice(total, part, (tap, 0, x, 16, 0))
        return total

    a_got = first_half(a0)
    a2, a3, b1, c1, *windows = together(*a_got, to(b0, "dev", OUTWARDS), to(c0, "dev", MIDDLE), *windows)
    b0, c0, a0 = jnp.where(end, b1, b0), c0 + c1, joined(a0, a_got)

    a_far = second_half(a0)
    b_got = first_half(b0)
    conv = conv_third(0, windows, taps)
    c1, b2, b3, *rest = together(to(c0, "dev", OUTWARDS), *b_got, *a_far, *conv)
    a_far, conv = rest[:2], rest[2:]
    c0, b0 = jnp.where(end, c1, c0), joined(b0, (b2, b3))

    b_far = second_half(b0)
    c_got = first_half(c0)
    conv = conv_third(1, windows, taps, conv)
    c1, c2, *rest = together(*c_got, *b_far, *conv)
    b_far, conv = rest[:2], rest[2:]
    c0 = joined(c0, (c1, c2))
    c_far = together(*second_half(c0))
    conv = conv_third(2, windows, taps, conv)

    kernel_grad = jnp.zeros((27, 2, 2, 32, channels), F32)
    kernel_grad = placed(kernel_grad, 9, a0, a_far)
    kernel_grad = placed(kernel_grad, 0, b0, b_far)
    kernel_grad = placed(kernel_grad, 18, c0, c_far)
    output, volume_grad = conv
    return output.reshape(volume.shape), volume_grad.reshape(volume.shape), kernel_grad.reshape(27, 128, channels).transpose(1, 0, 2)


def solution(mesh):
    sizes = tuple(mesh.shape[name] for name in ("dev", "ha", "wa"))
    placed = (P("dev", "ha", "wa", None), P(), P("dev", "ha", "wa", None))

    def per_device(volume, kernel, upstream):
        fits = sizes == (4, 4, 2) and volume.shape == (4, 8, 8, 256) and kernel.shape == (256, 27, 256)
        return (shared if fits else plain)(volume, kernel, upstream)

    return jax.shard_map(
        per_device,
        mesh=mesh,
        in_specs=placed,
        out_specs=(P("dev", "ha", "wa", None), P("dev", "ha", "wa", None), P("wa", None, None)),
        check_vma=False,
    )
```

```python
import functools
import math

import jax
import jax.numpy as jnp
from jax import lax
from jax.experimental import pallas as pl
from jax.experimental.pallas import tpu as pltpu
from jax.sharding import PartitionSpec as P

F32, BF16 = jnp.float32, jnp.bfloat16


def split(x):
    hi = x.astype(BF16)
    return hi, (x - hi.astype(F32)).astype(BF16)


def padded_by_halo(shard, sides):
    for axis, dim in sides:
        count, length = lax.axis_size(axis), shard.shape[dim]
        up = [(i, (i + 1) % count) for i in range(count)]
        down = [(j, i) for i, j in up]
        before = lax.ppermute(lax.slice_in_dim(shard, length - 1, length, axis=dim), axis, up)
        after = lax.ppermute(lax.slice_in_dim(shard, 0, 1, axis=dim), axis, down)
        shard = jnp.concatenate([before, shard, after], axis=dim)
    return shard


def plain(volume, kernel, upstream):
    depth, height, width, channels = volume.shape
    cells = depth * height * width
    padded = padded_by_halo(jnp.stack([volume, upstream]), (("dev", 1), ("ha", 2), ("wa", 3)))

    def windows(which, sign):
        return jnp.stack(
            [
                padded[which, 1 + sign * a :, 1 + sign * b :, 1 + sign * c :][:depth, :height, :width].reshape(cells, channels)
                for a in (-1, 0, 1) for b in (-1, 0, 1) for c in (-1, 0, 1)
            ],
            axis=1,
        )

    dot = functools.partial(jnp.einsum, precision=lax.Precision.HIGHEST, preferred_element_type=F32)
    forward, backward = windows(0, 1), windows(1, -1)
    output = dot("ntc,cto->no", forward, kernel)
    volume_grad = dot("nto,cto->nc", backward, kernel)
    total = cells * lax.axis_size("dev") * lax.axis_size("ha") * lax.axis_size("wa")
    summed = lax.psum(dot("ntc,no->cto", forward, upstream.reshape(cells, channels)) * (1.0 / math.sqrt(total)), ("dev", "ha", "wa"))
    owned = channels // lax.axis_size("wa")
    kernel_grad = lax.dynamic_slice_in_dim(summed, lax.axis_index("wa") * owned, owned, 0)
    return output.reshape(volume.shape), volume_grad.reshape(volume.shape), kernel_grad


def conv_kernel(a, *refs):
    v_refs, u_refs, k_ref, out_ref, grad_ref = refs[:3], refs[3:6], refs[6], refs[-2], refs[-1]
    b = pl.program_id(0)

    @pl.when(b == 0)
    def _():
        out_ref[...] = refs[7][...] if a else jnp.zeros_like(out_ref)
        grad_ref[...] = refs[8][...] if a else jnp.zeros_like(grad_ref)

    cells, channels = out_ref.shape
    d, h = v_refs[0].shape[0] - 2, v_refs[0].shape[1] - 2
    out, grad = out_ref[...], grad_ref[...]
    for c in range(3):
        k_hi, k_lo = split(k_ref[c])
        v_hi, v_lo = split(v_refs[c][a : a + d, pl.ds(b, h)].reshape(cells, channels))
        u_hi, u_lo = split(u_refs[2 - c][2 - a : 2 - a + d, pl.ds(2 - b, h)].reshape(cells, channels))
        for left, right in ((v_hi, k_hi), (v_hi, k_lo), (v_lo, k_hi)):
            out += jnp.dot(left, right, preferred_element_type=F32)
        for left, right in ((u_hi, k_hi), (u_hi, k_lo), (u_lo, k_hi)):
            grad += lax.dot_general(left, right, (((1,), (1,)), ((), ())), preferred_element_type=F32)
    out_ref[...] = out
    grad_ref[...] = grad


def shifted_3(padded):
    width = padded.shape[2] - 2
    return [padded[:, :, c : c + width] for c in range(3)]


def conv_third(a, windows, taps, before=()):
    planes, rows, width, channels = windows[0].shape
    cells = (planes - 2) * (rows - 2) * width
    whole = pl.BlockSpec((planes, rows, width, channels), lambda i: (0,) * 4)
    result = pl.BlockSpec((cells, channels), lambda i: (0, 0))
    shape = jax.ShapeDtypeStruct((cells, channels), F32)
    return pl.pallas_call(
        functools.partial(conv_kernel, a),
        grid=(3,),
        in_specs=[whole] * 6 + [pl.BlockSpec((3, channels, channels), lambda i: (3 * a + i, 0, 0))] + [result] * len(before),
        out_specs=[result, result],
        out_shape=[shape, shape],
        compiler_params=pltpu.CompilerParams(vmem_limit_bytes=40 * 2**20),
        cost_estimate=pl.CostEstimate(flops=2 * 6 * 9 * cells * channels * channels, bytes_accessed=4 * 2**20, transcendentals=0),
        name=f"conv_{a}",
    )(*windows, taps, *before)


def messages_kernel(below_ref, volume_ref, above_ref, *out_refs):
    h, w = lax.axis_index("ha"), lax.axis_index("wa")
    lane = lax.broadcasted_iota(jnp.int32, (64, 128), 1) // 32
    for t in range(3):
        tiles = []
        for z in (2 * t, 2 * t + 1):
            x = below_ref[0] if z == 0 else above_ref[0] if z == 5 else volume_ref[z - 1]
            left, right = x[:, :128], x[:, 128:]
            for tile in (jnp.where(w == 0, left, right), jnp.where(w == 0, right, left)):
                tiles.append(pltpu.roll(tile, lax.rem(128 - 32 * h, 128), 1))
        for k, out_ref in enumerate(out_refs):
            total = tiles[0] if k == 0 else pltpu.roll(tiles[0], 128 - 32 * k, 1)
            for j in range(1, 4):
                shift = 32 * (j - k) % 128
                total = jnp.where(lane == j, pltpu.roll(tiles[j], shift, 1) if shift else tiles[j], total)
            out_ref[:, 128 * t : 128 * t + 128] = total


def messages(below, volume, above):
    vmem = pl.BlockSpec(memory_space=pltpu.VMEM)
    return pl.pallas_call(
        messages_kernel,
        out_shape=[jax.ShapeDtypeStruct((64, 384), F32)] * 4,
        in_specs=[vmem] * 3,
        out_specs=[vmem] * 4,
        compiler_params=pltpu.CompilerParams(vmem_limit_bytes=4 * 2**20),
        name="messages",
    )(below, volume, above)


def lay_out(shifted, plane, first, second):
    lane = lax.broadcasted_iota(jnp.int32, (32, 8, 128), 2)
    row = lax.broadcasted_iota(jnp.int32, (32, 8, 128), 1)
    first = jnp.where(lane < 32, first, 0.0)
    second = jnp.where(lane < 32, second, 0.0)
    down_1, down_2 = pltpu.roll(first, 1, 1), pltpu.roll(second, 1, 1)
    up_1, up_2 = pltpu.roll(first, 7, 1), pltpu.roll(second, 7, 1)
    for w, (before, here, after) in enumerate(
        (
            (jnp.where(row == 0, down_2, down_1), first, jnp.where(row == 7, up_2, up_1)),
            (jnp.where(row == 0, down_1, down_2), second, jnp.where(row == 7, up_1, up_2)),
        )
    ):
        joined = before + pltpu.roll(here, 32, 2) + pltpu.roll(after, 64, 2)
        shifted[w, plane, pl.ds(1, 32)] = joined
        shifted[w, plane, 0] = joined[31]
        shifted[w, plane, 33] = joined[0]


def plane_of(refs, z, offset):
    tile = 128 * (z // 2)
    plane = jnp.concatenate([ref[:, tile : tile + 128].reshape(8, 8, 128) for ref in refs], axis=0)
    return pltpu.roll(plane, (128 - 64 * (z % 2) - offset) % 128, 2)


def plane_grad_kernel(scale, planes, *refs):
    u_refs, mine, other, out_refs, shifted, u_cat = refs[:8], refs[8:12], refs[12:16], refs[16:-2], refs[-2], refs[-1]
    share = out_refs[0].shape[0]
    for z in range(1, 5) if planes == (1,) else range(6):
        lay_out(shifted, z, plane_of(mine, z, 0), plane_of(other, z, 32))
    for i, ref in enumerate(u_refs):
        hi, lo = split(ref[...].T)
        u_cat[i, :, 0:256] = hi
        u_cat[i, :, 256:512] = hi
        u_cat[i, :, 512:768] = lo
    windows = [(a, b) for a in planes for b in range(3)]
    for start in range(0, len(windows), 2):
        group = windows[start : start + 2]
        total = jnp.zeros((256, 128 * len(group)), F32)
        for w in range(2):
            for k in range(4):
                cells = [shifted[w, a : a + 4, 8 * k + b : 8 * k + b + 8].reshape(256, 128) for a, b in group]
                hi, lo = split(jnp.concatenate(cells, axis=1))
                right = jnp.concatenate([hi, lo, hi], axis=0)
                total += jnp.dot(u_cat[4 * w + k], right, preferred_element_type=F32)
        turned = total.T * scale
        for i in range(len(group)):
            for c in range(3):
                tap = 3 * (start + i) + c
                out_refs[tap // share][tap % share] = turned[128 * i + 32 * c : 128 * i + 32 * c + 32]


def plane_grad(scale, planes, pieces, blocks):
    vmem = pl.BlockSpec(memory_space=pltpu.VMEM)
    return pl.pallas_call(
        functools.partial(plane_grad_kernel, scale, planes),
        out_shape=[jax.ShapeDtypeStruct((9 * len(planes) // pieces, 32, 256), F32)] * pieces,
        in_specs=[vmem] * 16,
        out_specs=[vmem] * pieces,
        scratch_shapes=[pltpu.VMEM((2, 6, 34, 8, 128), F32), pltpu.VMEM((8, 256, 768), BF16)],
        compiler_params=pltpu.CompilerParams(vmem_limit_bytes=40 * 2**20),
        cost_estimate=pl.CostEstimate(flops=2 * 3 * 9 * len(planes) * 32 * 2048 * 256, bytes_accessed=4 * 2**20, transcendentals=0),
        name=f"plane_grad_{len(planes)}",
    )(*blocks)


def placed_kernel(firsts, *refs):
    pieces, out_ref, sems = refs[: 4 * len(firsts)], refs[-2], refs[-1]
    h = lax.axis_index("ha")
    copies = []
    for i, ref in enumerate(pieces):
        last = i % 2
        near, far = (2, 1) if last else (1, 2)
        for j in range(2):
            chip = h ^ (near * j + (far if i % 4 >= 2 else 0))
            rows = pl.ds(pl.multiple_of(32 * chip + 16 * last, 16), 16)
            copies.append(pltpu.make_async_copy(ref.at[j], out_ref.at[pl.ds(firsts[i // 4], ref.shape[1]), rows], sems.at[len(copies)]))
            copies[-1].start()
    for copy in copies:
        copy.wait()


def placed(firsts, pieces, total=None):
    vmem, hbm = pl.BlockSpec(memory_space=pltpu.VMEM), pl.BlockSpec(memory_space=pltpu.HBM)
    more = [] if total is None else [total]
    return pl.pallas_call(
        functools.partial(placed_kernel, firsts),
        out_shape=jax.ShapeDtypeStruct((27, 128, 256), F32),
        in_specs=[vmem] * len(pieces) + [hbm] * len(more),
        out_specs=hbm,
        scratch_shapes=[pltpu.SemaphoreType.DMA((2 * len(pieces),))],
        input_output_aliases={len(pieces): 0} if more else {},
        compiler_params=pltpu.CompilerParams(vmem_limit_bytes=4 * 2**20),
        name=f"placed_{len(firsts)}",
    )(*pieces, *more)


SWAP = [(0, 1), (1, 0)]
UP = [(i, (i + 1) % 4) for i in range(4)]
DOWN = [((i + 1) % 4, i) for i in range(4)]


def pair(bit):
    return [(i, i ^ bit) for i in range(4)]


INWARDS, MIDDLE, OUTWARDS = [(0, 1), (3, 2)], [(1, 2), (2, 1)], [(1, 0), (2, 3)]


def together(*arrays):
    return lax.optimization_barrier(arrays)


def to(x, axis, where):
    return lax.ppermute(x, axis, where)


def shared(volume, kernel, upstream):
    h, w = lax.axis_index("ha"), lax.axis_index("wa")
    channels = volume.shape[-1]
    taps = kernel.transpose(1, 0, 2)
    scale = 1.0 / math.sqrt(256 * 32)

    z = lax.axis_index("dev")
    end = (z == 0) | (z == 3)

    def around(messages):
        return [messages[0]] + [to(messages[4 - k], "ha", [((i + k) % 4, i) for i in range(4)]) for k in (1, 2, 3)]

    u_mine = around([upstream.reshape(256, channels)] * 4)
    u_other = [to(u_mine[0], "wa", SWAP)]
    volume, upstream, u_other[0] = together(volume, upstream, u_other[0])
    below = to(jnp.stack([volume[3], upstream[3]]), "dev", UP)
    above = to(jnp.stack([volume[0], upstream[0]]), "dev", DOWN)
    parts = messages(below.reshape(2, 64, channels), volume.reshape(4, 64, channels), above.reshape(2, 64, channels))
    v_mine = around(parts)
    *arrived, _ = together(*u_mine[1:], parts[0])
    u_mine = u_mine[:1] + arrived
    u_other += [to(x, "wa", SWAP) for x in arrived]
    v_other = [to(x, "wa", SWAP) for x in v_mine]
    blocks = [*u_mine, *u_other, *v_mine, *v_other]

    (a0,) = plane_grad(scale, (1,), 1, blocks)

    a1 = to(a0, "dev", INWARDS)
    b0, c0 = plane_grad(scale, (0, 2), 2, blocks)
    b1, c1 = to(b0, "dev", INWARDS), to(c0, "dev", INWARDS)
    a0, b0 = together(a0 + a1, b0)
    a1 = to(a0, "dev", MIDDLE)
    a1, b1 = together(a1, b1)
    a0, b0 = a0 + a1, b0 + b1

    def edge(row):
        return jnp.concatenate([below[:, row : row + 1], volume[:, row : row + 1], above[:, row : row + 1]], axis=0)

    low_edge, high_edge, b0 = together(edge(0), edge(7), b0)
    behind, ahead = to(high_edge, "ha", UP), to(low_edge, "ha", DOWN)
    a1, b1 = to(a0, "dev", OUTWARDS), to(b0, "dev", MIDDLE)
    a1, b1, c1, behind, ahead = together(a1, b1, c1, behind, ahead)
    a0, b0, c0 = jnp.where(end, a1, a0), b0 + b1, c0 + c1
    deep = jnp.concatenate([below, volume, above], axis=0)
    rows = jnp.concatenate([behind, deep, ahead], axis=1)
    v_rows = jnp.concatenate([rows[0:1], rows[2:7]], axis=0)
    u_own = [x.reshape(4, 8, 8, channels) for x in u_mine]
    u_rows = jnp.concatenate([u_own[3][:, 7:8], u_own[0], u_own[1][:, 0:1]], axis=1)
    u_rows = jnp.concatenate([rows[1:2], u_rows, rows[7:8]], axis=0)
    both = jnp.concatenate([v_rows, u_rows], axis=0)
    sides = to(jnp.concatenate([both[:, :, 7:8], both[:, :, 0:1]], axis=2), "wa", SWAP)
    both = jnp.concatenate([sides[:, :, 0:1], both, sides[:, :, 1:2]], axis=2)
    windows = shifted_3(both[:6]) + shifted_3(both[6:])

    def first_half(x):
        return to(x[:, :16], "ha", pair(1)), to(x[:, 16:], "ha", pair(2))

    def joined(x, got):
        return jnp.stack([x[:, :16], got[0]]), jnp.stack([x[:, 16:], got[1]])

    def second_half(x):
        return to(x[0], "ha", pair(2)), to(x[1], "ha", pair(1))

    a_got = first_half(a0)
    a2, a3, b1, c1, *windows = together(*a_got, to(b0, "dev", OUTWARDS), to(c0, "dev", MIDDLE), *windows)
    b0, c0, a0 = jnp.where(end, b1, b0), c0 + c1, joined(a0, a_got)

    a_far = second_half(a0)
    b_got = first_half(b0)
    conv = conv_third(0, windows, taps)
    c1, b2, b3, *rest = together(to(c0, "dev", OUTWARDS), *b_got, *a_far, *conv)
    a_far, conv = rest[:2], rest[2:]
    c0, b0 = jnp.where(end, c1, c0), joined(b0, (b2, b3))

    b_far = second_half(b0)
    c_got = first_half(c0)
    conv = conv_third(1, windows, taps, conv)
    c1, c2, *rest = together(*c_got, *b_far, *conv)
    b_far, conv = rest[:2], rest[2:]
    c0 = joined(c0, (c1, c2))
    c_far = together(*second_half(c0))
    conv = conv_third(2, windows, taps, conv)

    kernel_grad = placed((9, 0), (*a0, *a_far, *b0, *b_far))
    kernel_grad = placed((18,), (*c0, *c_far), kernel_grad)
    output, volume_grad = conv
    return output.reshape(volume.shape), volume_grad.reshape(volume.shape), kernel_grad.transpose(1, 0, 2)


def solution(mesh):
    sizes = tuple(mesh.shape[name] for name in ("dev", "ha", "wa"))
    placed = (P("dev", "ha", "wa", None), P(), P("dev", "ha", "wa", None))

    def per_device(volume, kernel, upstream):
        fits = sizes == (4, 4, 2) and volume.shape == (4, 8, 8, 256) and kernel.shape == (256, 27, 256)
        return (shared if fits else plain)(volume, kernel, upstream)

    return jax.shard_map(
        per_device,
        mesh=mesh,
        in_specs=placed,
        out_specs=(P("dev", "ha", "wa", None), P("dev", "ha", "wa", None), P("wa", None, None)),
        check_vma=False,
    )
```

```python
import functools
import math

import jax
import jax.numpy as jnp
from jax import lax
from jax.experimental import pallas as pl
from jax.experimental.pallas import tpu as pltpu
from jax.sharding import PartitionSpec as P

F32, BF16 = jnp.float32, jnp.bfloat16


def split(x):
    hi = x.astype(BF16)
    return hi, (x - hi.astype(F32)).astype(BF16)


def padded_by_halo(shard, sides):
    for axis, dim in sides:
        count, length = lax.axis_size(axis), shard.shape[dim]
        up = [(i, (i + 1) % count) for i in range(count)]
        down = [(j, i) for i, j in up]
        before = lax.ppermute(lax.slice_in_dim(shard, length - 1, length, axis=dim), axis, up)
        after = lax.ppermute(lax.slice_in_dim(shard, 0, 1, axis=dim), axis, down)
        shard = jnp.concatenate([before, shard, after], axis=dim)
    return shard


def plain(volume, kernel, upstream):
    depth, height, width, channels = volume.shape
    cells = depth * height * width
    padded = padded_by_halo(jnp.stack([volume, upstream]), (("dev", 1), ("ha", 2), ("wa", 3)))

    def windows(which, sign):
        return jnp.stack(
            [
                padded[which, 1 + sign * a :, 1 + sign * b :, 1 + sign * c :][:depth, :height, :width].reshape(cells, channels)
                for a in (-1, 0, 1) for b in (-1, 0, 1) for c in (-1, 0, 1)
            ],
            axis=1,
        )

    dot = functools.partial(jnp.einsum, precision=lax.Precision.HIGHEST, preferred_element_type=F32)
    forward, backward = windows(0, 1), windows(1, -1)
    output = dot("ntc,cto->no", forward, kernel)
    volume_grad = dot("nto,cto->nc", backward, kernel)
    total = cells * lax.axis_size("dev") * lax.axis_size("ha") * lax.axis_size("wa")
    summed = lax.psum(dot("ntc,no->cto", forward, upstream.reshape(cells, channels)) * (1.0 / math.sqrt(total)), ("dev", "ha", "wa"))
    owned = channels // lax.axis_size("wa")
    kernel_grad = lax.dynamic_slice_in_dim(summed, lax.axis_index("wa") * owned, owned, 0)
    return output.reshape(volume.shape), volume_grad.reshape(volume.shape), kernel_grad


def conv_kernel(a, *refs):
    v_refs, u_refs, k_ref, out_ref, grad_ref = refs[:3], refs[3:6], refs[6], refs[-2], refs[-1]
    b = pl.program_id(0)

    @pl.when(b == 0)
    def _():
        out_ref[...] = refs[7][...] if a else jnp.zeros_like(out_ref)
        grad_ref[...] = refs[8][...] if a else jnp.zeros_like(grad_ref)

    cells, channels = out_ref.shape
    d, h = v_refs[0].shape[0] - 2, v_refs[0].shape[1] - 2
    out, grad = out_ref[...], grad_ref[...]
    for c in range(3):
        k_hi, k_lo = split(k_ref[c])
        v_hi, v_lo = split(v_refs[c][a : a + d, pl.ds(b, h)].reshape(cells, channels))
        u_hi, u_lo = split(u_refs[2 - c][2 - a : 2 - a + d, pl.ds(2 - b, h)].reshape(cells, channels))
        for left, right in ((v_hi, k_hi), (v_hi, k_lo), (v_lo, k_hi)):
            out += jnp.dot(left, right, preferred_element_type=F32)
        for left, right in ((u_hi, k_hi), (u_hi, k_lo), (u_lo, k_hi)):
            grad += lax.dot_general(left, right, (((1,), (1,)), ((), ())), preferred_element_type=F32)
    out_ref[...] = out
    grad_ref[...] = grad


def shifted_3(padded):
    width = padded.shape[2] - 2
    return [padded[:, :, c : c + width] for c in range(3)]


def conv_third(a, windows, taps, before=()):
    planes, rows, width, channels = windows[0].shape
    cells = (planes - 2) * (rows - 2) * width
    whole = pl.BlockSpec((planes, rows, width, channels), lambda i: (0,) * 4)
    result = pl.BlockSpec((cells, channels), lambda i: (0, 0))
    shape = jax.ShapeDtypeStruct((cells, channels), F32)
    return pl.pallas_call(
        functools.partial(conv_kernel, a),
        grid=(3,),
        in_specs=[whole] * 6 + [pl.BlockSpec((3, channels, channels), lambda i: (3 * a + i, 0, 0))] + [result] * len(before),
        out_specs=[result, result],
        out_shape=[shape, shape],
        compiler_params=pltpu.CompilerParams(vmem_limit_bytes=40 * 2**20),
        cost_estimate=pl.CostEstimate(flops=2 * 6 * 9 * cells * channels * channels, bytes_accessed=4 * 2**20, transcendentals=0),
        name=f"conv_{a}",
    )(*windows, taps, *before)


def messages_kernel(*refs):
    h, w = lax.axis_index("ha"), lax.axis_index("wa")
    lane = lax.broadcasted_iota(jnp.int32, (64, 128), 1) // 32
    out_refs = refs[-4:]
    own = len(refs) == 7
    if own:
        refs[2][...] = refs[1][...]
        pairs = [(refs[0][0], refs[0][1]), (refs[0][2], refs[0][3])]
    else:
        pairs = [(refs[0][0], refs[1][0])]
        for out_ref, there_ref in zip(out_refs, refs[2:6]):
            out_ref[:, :256] = there_ref[...]
    for t, pair_of_planes in enumerate(pairs, 0 if own else 2):
        tiles = []
        for x in pair_of_planes:
            left, right = x[:, :128], x[:, 128:]
            for tile in (jnp.where(w == 0, left, right), jnp.where(w == 0, right, left)):
                tiles.append(pltpu.roll(tile, lax.rem(128 - 32 * h, 128), 1))
        for k, out_ref in enumerate(out_refs):
            total = tiles[0] if k == 0 else pltpu.roll(tiles[0], 128 - 32 * k, 1)
            for j in range(1, 4):
                shift = 32 * (j - k) % 128
                total = jnp.where(lane == j, pltpu.roll(tiles[j], shift, 1) if shift else tiles[j], total)
            out_ref[:, 128 * t : 128 * t + 128] = total


def messages(lanes, *arrays):
    vmem = pl.BlockSpec(memory_space=pltpu.VMEM)
    shapes = [jax.ShapeDtypeStruct((64, lanes), F32)] * 4
    if lanes == 256:
        shapes = [jax.ShapeDtypeStruct(arrays[1].shape, F32), *shapes]
    return pl.pallas_call(
        messages_kernel,
        out_shape=shapes,
        in_specs=[vmem] * len(arrays),
        out_specs=[vmem] * len(shapes),
        compiler_params=pltpu.CompilerParams(vmem_limit_bytes=4 * 2**20),
        name=f"messages_{lanes}",
    )(*arrays)


def lay_out(shifted, plane, first, second):
    lane = lax.broadcasted_iota(jnp.int32, (32, 8, 128), 2)
    row = lax.broadcasted_iota(jnp.int32, (32, 8, 128), 1)
    first = jnp.where(lane < 32, first, 0.0)
    second = jnp.where(lane < 32, second, 0.0)
    down_1, down_2 = pltpu.roll(first, 1, 1), pltpu.roll(second, 1, 1)
    up_1, up_2 = pltpu.roll(first, 7, 1), pltpu.roll(second, 7, 1)
    for w, (before, here, after) in enumerate(
        (
            (jnp.where(row == 0, down_2, down_1), first, jnp.where(row == 7, up_2, up_1)),
            (jnp.where(row == 0, down_1, down_2), second, jnp.where(row == 7, up_1, up_2)),
        )
    ):
        joined = before + pltpu.roll(here, 32, 2) + pltpu.roll(after, 64, 2)
        shifted[w, plane, pl.ds(1, 32)] = joined
        shifted[w, plane, 0] = joined[31]
        shifted[w, plane, 33] = joined[0]


def plane_of(refs, z, offset):
    z = (1, 2, 3, 4, 0, 5).index(z)
    tile = 128 * (z // 2)
    plane = jnp.concatenate([ref[:, tile : tile + 128].reshape(8, 8, 128) for ref in refs], axis=0)
    return pltpu.roll(plane, (128 - 64 * (z % 2) - offset) % 128, 2)


def plane_grad_kernel(scale, planes, *refs):
    u_refs, mine, other, out_refs, shifted, u_cat = refs[:8], refs[8:12], refs[12:16], refs[16:-2], refs[-2], refs[-1]
    share = out_refs[0].shape[0]
    for z in range(1, 5) if planes == (1,) else range(6):
        lay_out(shifted, z, plane_of(mine, z, 0), plane_of(other, z, 32))
    for i, ref in enumerate(u_refs):
        hi, lo = split(ref[...].T)
        u_cat[i, :, 0:256] = hi
        u_cat[i, :, 256:512] = hi
        u_cat[i, :, 512:768] = lo
    windows = [(a, b) for a in planes for b in range(3)]
    for start in range(0, len(windows), 2):
        group = windows[start : start + 2]
        total = jnp.zeros((256, 128 * len(group)), F32)
        for w in range(2):
            for k in range(4):
                cells = [shifted[w, a : a + 4, 8 * k + b : 8 * k + b + 8].reshape(256, 128) for a, b in group]
                hi, lo = split(jnp.concatenate(cells, axis=1))
                right = jnp.concatenate([hi, lo, hi], axis=0)
                total += jnp.dot(u_cat[4 * w + k], right, preferred_element_type=F32)
        turned = total.T * scale
        for i in range(len(group)):
            for c in range(3):
                tap = 3 * (start + i) + c
                out_refs[tap // share][tap % share] = turned[128 * i + 32 * c : 128 * i + 32 * c + 32]


def plane_grad(scale, planes, pieces, blocks):
    vmem = pl.BlockSpec(memory_space=pltpu.VMEM)
    return pl.pallas_call(
        functools.partial(plane_grad_kernel, scale, planes),
        out_shape=[jax.ShapeDtypeStruct((9 * len(planes) // pieces, 32, 256), F32)] * pieces,
        in_specs=[vmem] * 16,
        out_specs=[vmem] * pieces,
        scratch_shapes=[pltpu.VMEM((2, 6, 34, 8, 128), F32), pltpu.VMEM((8, 256, 768), BF16)],
        compiler_params=pltpu.CompilerParams(vmem_limit_bytes=40 * 2**20),
        cost_estimate=pl.CostEstimate(flops=2 * 3 * 9 * len(planes) * 32 * 2048 * 256, bytes_accessed=4 * 2**20, transcendentals=0),
        name=f"plane_grad_{len(planes)}",
    )(*blocks)


def placed_kernel(firsts, *refs):
    pieces, out_ref, sems = refs[: 4 * len(firsts)], refs[-2], refs[-1]
    h = lax.axis_index("ha")
    copies = []
    for i, ref in enumerate(pieces):
        last = i % 2
        near, far = (2, 1) if last else (1, 2)
        for j in range(2):
            chip = h ^ (near * j + (far if i % 4 >= 2 else 0))
            rows = pl.ds(pl.multiple_of(32 * chip + 16 * last, 16), 16)
            copies.append(pltpu.make_async_copy(ref.at[j], out_ref.at[pl.ds(firsts[i // 4], ref.shape[1]), rows], sems.at[len(copies)]))
            copies[-1].start()
    for copy in copies:
        copy.wait()


def placed(firsts, pieces, total=None):
    vmem, hbm = pl.BlockSpec(memory_space=pltpu.VMEM), pl.BlockSpec(memory_space=pltpu.HBM)
    more = [] if total is None else [total]
    return pl.pallas_call(
        functools.partial(placed_kernel, firsts),
        out_shape=jax.ShapeDtypeStruct((27, 128, 256), F32),
        in_specs=[vmem] * len(pieces) + [hbm] * len(more),
        out_specs=hbm,
        scratch_shapes=[pltpu.SemaphoreType.DMA((2 * len(pieces),))],
        input_output_aliases={len(pieces): 0} if more else {},
        compiler_params=pltpu.CompilerParams(vmem_limit_bytes=4 * 2**20),
        name=f"placed_{len(firsts)}",
    )(*pieces, *more)


SWAP = [(0, 1), (1, 0)]
UP = [(i, (i + 1) % 4) for i in range(4)]
DOWN = [((i + 1) % 4, i) for i in range(4)]


def pair(bit):
    return [(i, i ^ bit) for i in range(4)]


INWARDS, MIDDLE, OUTWARDS = [(0, 1), (3, 2)], [(1, 2), (2, 1)], [(1, 0), (2, 3)]


def together(*arrays):
    return lax.optimization_barrier(arrays)


def to(x, axis, where):
    return lax.ppermute(x, axis, where)


def shared(volume, kernel, upstream):
    h, w = lax.axis_index("ha"), lax.axis_index("wa")
    channels = volume.shape[-1]
    taps = kernel.transpose(1, 0, 2)
    scale = 1.0 / math.sqrt(256 * 32)

    z = lax.axis_index("dev")
    end = (z == 0) | (z == 3)

    def around(messages):
        return [messages[0]] + [to(messages[4 - k], "ha", [((i + k) % 4, i) for i in range(4)]) for k in (1, 2, 3)]

    u_mine = around([upstream.reshape(256, channels)] * 4)
    u_other = [to(u_mine[0], "wa", SWAP)]
    own, *parts = messages(256, volume.reshape(4, 64, channels), u_mine[0])
    volume, upstream, u_other[0] = together(volume, upstream, u_other[0])
    below = to(jnp.stack([volume[3], upstream[3]]), "dev", UP)
    above = to(jnp.stack([volume[0], upstream[0]]), "dev", DOWN)
    parts = messages(384, below.reshape(2, 64, channels), above.reshape(2, 64, channels), *parts)
    v_mine = around(parts)
    *arrived, _ = together(*u_mine[1:], parts[0])
    u_mine = u_mine[:1] + arrived
    u_other += [to(x, "wa", SWAP) for x in arrived]
    v_other = [to(x, "wa", SWAP) for x in v_mine]
    blocks = [own, *u_mine[1:], *u_other, *v_mine, *v_other]

    (a0,) = plane_grad(scale, (1,), 1, blocks)

    a1 = to(a0, "dev", INWARDS)
    b0, c0 = plane_grad(scale, (0, 2), 2, blocks)
    b1, c1 = to(b0, "dev", INWARDS), to(c0, "dev", INWARDS)
    a0, b0 = together(a0 + a1, b0)
    a1 = to(a0, "dev", MIDDLE)
    a1, b1 = together(a1, b1)
    a0, b0 = a0 + a1, b0 + b1

    def edge(row):
        return jnp.concatenate([below[:, row : row + 1], volume[:, row : row + 1], above[:, row : row + 1]], axis=0)

    low_edge, high_edge, b0 = together(edge(0), edge(7), b0)
    behind, ahead = to(high_edge, "ha", UP), to(low_edge, "ha", DOWN)
    a1, b1 = to(a0, "dev", OUTWARDS), to(b0, "dev", MIDDLE)
    a1, b1, c1, behind, ahead = together(a1, b1, c1, behind, ahead)
    a0, b0, c0 = jnp.where(end, a1, a0), b0 + b1, c0 + c1
    deep = jnp.concatenate([below, volume, above], axis=0)
    rows = jnp.concatenate([behind, deep, ahead], axis=1)
    v_rows = jnp.concatenate([rows[0:1], rows[2:7]], axis=0)
    u_own = [x.reshape(4, 8, 8, channels) for x in u_mine]
    u_rows = jnp.concatenate([u_own[3][:, 7:8], u_own[0], u_own[1][:, 0:1]], axis=1)
    u_rows = jnp.concatenate([rows[1:2], u_rows, rows[7:8]], axis=0)
    both = jnp.concatenate([v_rows, u_rows], axis=0)
    sides = to(jnp.concatenate([both[:, :, 7:8], both[:, :, 0:1]], axis=2), "wa", SWAP)
    both = jnp.concatenate([sides[:, :, 0:1], both, sides[:, :, 1:2]], axis=2)
    windows = shifted_3(both[:6]) + shifted_3(both[6:])

    def first_half(x):
        return to(x[:, :16], "ha", pair(1)), to(x[:, 16:], "ha", pair(2))

    def joined(x, got):
        return jnp.stack([x[:, :16], got[0]]), jnp.stack([x[:, 16:], got[1]])

    def second_half(x):
        return to(x[0], "ha", pair(2)), to(x[1], "ha", pair(1))

    a_got = first_half(a0)
    a2, a3, b1, c1, *windows = together(*a_got, to(b0, "dev", OUTWARDS), to(c0, "dev", MIDDLE), *windows)
    b0, c0, a0 = jnp.where(end, b1, b0), c0 + c1, joined(a0, a_got)

    a_far = second_half(a0)
    b_got = first_half(b0)
    conv = conv_third(0, windows, taps)
    c1, b2, b3, *rest = together(to(c0, "dev", OUTWARDS), *b_got, *a_far, *conv)
    a_far, conv = rest[:2], rest[2:]
    c0, b0 = jnp.where(end, c1, c0), joined(b0, (b2, b3))

    b_far = second_half(b0)
    c_got = first_half(c0)
    conv = conv_third(1, windows, taps, conv)
    c1, c2, *rest = together(*c_got, *b_far, *conv)
    b_far, conv = rest[:2], rest[2:]
    c0 = joined(c0, c_got)
    c_far = together(*second_half(c0))
    conv = conv_third(2, windows, taps, conv)

    kernel_grad = placed((9, 0), (*a0, *a_far, *b0, *b_far))
    kernel_grad = placed((18,), (*c0, *c_far), kernel_grad)
    output, volume_grad = conv
    return output.reshape(volume.shape), volume_grad.reshape(volume.shape), kernel_grad.transpose(1, 0, 2)


def solution(mesh):
    sizes = tuple(mesh.shape[name] for name in ("dev", "ha", "wa"))
    placed = (P("dev", "ha", "wa", None), P(), P("dev", "ha", "wa", None))

    def per_device(volume, kernel, upstream):
        fits = sizes == (4, 4, 2) and volume.shape == (4, 8, 8, 256) and kernel.shape == (256, 27, 256)
        return (shared if fits else plain)(volume, kernel, upstream)

    return jax.shard_map(
        per_device,
        mesh=mesh,
        in_specs=placed,
        out_specs=(P("dev", "ha", "wa", None), P("dev", "ha", "wa", None), P("wa", None, None)),
        check_vma=False,
    )
```
